256 devices in a mesh: chan: 8 (over y_lo, x), ctx: 32 (over z, y_hi, core).
Axes of the slice: x: 4, y: 4 (y_hi: 2, y_lo: 2; y = y_hi * 2 + y_lo), z: 8, core: 2. Of those that a mesh axis runs over, the one named last changes fastest.
Arguments:
- value: bfloat16 [16384, 4096], P('ctx', 'chan'), may hold values from -6 to 6
- gate_in: bfloat16 [16384, 4096], P('ctx', 'chan'), may hold values from -6 to 6
- gate_out: bfloat16 [16384, 4096], P('ctx', 'chan'), may hold values from -6 to 6
- filt: bfloat16 [16384, 4096], P('ctx', 'chan'), may hold values from -0.046875 to 0.046875
- skip: float32 [4096], P('chan'), may hold values from -1 to 1
- w_out: bfloat16 [4096, 4096], P('chan'), may hold values from -0.125 to 0.125
Outputs:
- layer_out: bfloat16 [16384, 4096], P('ctx', 'chan')
The draws below stay inside these ranges and needn't reach their ends.
All inputs are finite; a program needn't handle non-finite values.
Results may differ from the reference program's by a relative error of at most 0.0058.
Values may be sent and summed in bfloat16 or wider, within the bound.
No kernel may reach another device: no remote copies, remote signals or barrier semaphores. Data moves between devices by JAX's collectives and lax.ppermute only.
A program may use at most 128 MiB of HBM per device.

```python
import jax
import jax.numpy as jnp
from jax import lax

D = 4096
SEQ = 16384


def with_spikes(result, rng, source, target, blocks, factor):
    owner, partner = [(jnp.arange(result.shape[dim]) // (result.shape[dim] // blocks)).reshape([-1 if axis == dim else 1 for axis in range(result.ndim)]) for dim in (source, target)]
    chosen = jax.random.permutation(rng, blocks)[partner]
    strong = (owner == chosen) | (owner == (partner + blocks // 2) % blocks)
    return jnp.where(strong, factor * result, result)


def shard_levels(key, extent, split, smallest, high):
    def one(position, parts):
        heights = jax.random.uniform(jax.random.fold_in(jax.random.fold_in(key, 6), position), (parts,), jnp.float32, smallest / len(split), high / len(split))
        return jnp.repeat(jnp.exp(heights), extent[position] // parts).reshape((-1,) + (1,) * (len(extent) - position - 1))

    level = one(*split[0])
    for cut in split[1:]:
        level = level * one(*cut)
    return level


def noise(stream_key, extent, deviation, most, shards=(), held_as=jnp.bfloat16):
    values = deviation * jax.random.normal(stream_key, extent, jnp.float32)
    if shards:
        values = values * shard_levels(stream_key, extent, shards, -0.22, 0.18)
    return jnp.clip(values, -most, most).astype(held_as)


def heavy_noise(rng, shape, scale, most, shards, heavy, dtype=jnp.bfloat16):
    result = scale * jax.random.normal(rng, shape, jnp.float32)
    if shards:
        result = result * shard_levels(rng, shape, shards, -0.22, 0.18)
    return jnp.clip(with_spikes(result, jax.random.fold_in(rng, 3), *heavy), -most, most).astype(dtype)


def setup_inputs(seed: int = 0) -> dict:
    splits = jax.random.split(jax.random.key(seed), 7)
    return {
        "value": noise(splits[0], (SEQ, D), 1.0, 6.0, ((0, 32), (1, 8))),
        "gate_in": noise(splits[1], (SEQ, D), 1.0, 6.0, ((0, 32), (1, 8))),
        "gate_out": noise(splits[2], (SEQ, D), 1.0, 6.0, ((0, 32), (1, 8))),
        "filt": noise(splits[3], (SEQ, D), SEQ ** -0.5, 0.046875, ((0, 32), (1, 8))),
        "skip": jnp.clip(jax.random.uniform(splits[4], (D,), jnp.float32, -1.0, 1.0) * shard_levels(splits[4], (D,), ((0, 8),), -0.4, 0.0), -1.0, 1.0),
        "w_out": heavy_noise(splits[5], (D, D), D ** -0.5, 0.125, ((0, 8),), (0, 1, 8, 2.0)),
    }


def reference(value, gate_in, gate_out, filt, skip, w_out):
    gated = (gate_in.astype(jnp.float32) * value.astype(jnp.float32)).astype(jnp.bfloat16)
    length, width = gated.shape
    block_width = min(256, width)
    count = width // block_width
    signal = gated.astype(jnp.float32).reshape(length, count, block_width).transpose(1, 0, 2)
    response = filt.astype(jnp.float32).reshape(length, count, block_width).transpose(1, 0, 2)

    def convolve(pair):
        first, second = pair
        spectrum = jnp.fft.rfft(first, n=2 * length, axis=0) * jnp.fft.rfft(second, n=2 * length, axis=0)
        return jnp.fft.irfft(spectrum, n=2 * length, axis=0)[:length].astype(jnp.float32)

    conv = lax.map(convolve, (signal, response)).transpose(1, 0, 2).reshape(length, width)
    inner = conv + skip.astype(jnp.float32)[None, :] * gated.astype(jnp.float32)
    mixed = (gate_out.astype(jnp.float32) * inner).astype(jnp.bfloat16)
    return jnp.dot(mixed, w_out, preferred_element_type=jnp.float32).astype(jnp.bfloat16)
```

```python
import functools

import jax
import jax.numpy as jnp
import numpy as np
from jax import lax
from jax.experimental import pallas as pl
from jax.experimental.pallas import tpu as pltpu
from jax.sharding import PartitionSpec as P

EDGE = 128
VMEM = 48 * 1024 * 1024


def split_table(table):
    high = table.astype(jnp.bfloat16)
    low = (table - high.astype(np.float64)).astype(jnp.bfloat16)
    return high, low


@functools.cache
def transform_tables():
    steps = np.arange(EDGE)
    slow = 2.0 * np.pi * np.outer(steps + 0.25, steps) / EDGE
    fast = 2.0 * np.pi * np.outer(steps, steps) / EDGE
    turn = 2.0 * np.pi * np.outer(steps + 0.25, steps) / (EDGE * EDGE)
    first = np.concatenate([np.cos(slow), -np.sin(slow)], 0)
    second = np.block([[np.cos(fast), -np.sin(fast)], [np.sin(fast), np.cos(fast)]])
    third = np.block([[np.cos(fast), np.sin(fast)], [-np.sin(fast), np.cos(fast)]]) / EDGE
    last = np.concatenate([np.cos(slow).T, -np.sin(slow).T], 1) / EDGE
    first_high, first_low = split_table(first)
    return (
        np.concatenate([first_high, first_low], 1),
        np.cos(turn).astype(np.float32),
        np.sin(turn).astype(np.float32),
        *split_table(second),
        *split_table(third),
        *split_table(last),
    )


def halves(array):
    high = array.astype(jnp.bfloat16)
    return high, (array - high.astype(jnp.float32)).astype(jnp.bfloat16)


def dot(a, b):
    return jnp.dot(a, b, preferred_element_type=jnp.float32)


def pack_kernel(value_ref, gate_ref, filt_ref, out_ref):
    gated = (gate_ref[...].astype(jnp.float32) * value_ref[...].astype(jnp.float32)).astype(
        jnp.bfloat16
    )
    chans = out_ref.shape[3]
    peers = EDGE // chans
    for which, array in enumerate((gated, filt_ref[...])):
        for part in range(array.shape[1] // EDGE):
            turned = array[:, part * EDGE : (part + 1) * EDGE].T
            out_ref[part * peers : (part + 1) * peers, 0, which] = turned.reshape(
                peers, chans, EDGE
            )


def conv_kernel(
    chans, in_ref, w1, cos_ref, sin_ref, w2h, w2l, w3h, w3l, w4h, w4l, out_ref, wide, back
):
    wide[...] = in_ref[...].astype(jnp.float32)
    cos, sin = cos_ref[...], sin_ref[...]

    @pl.loop(0, chans)
    def _(chan):
        both = jnp.concatenate(
            [
                wide[pl.ds(which * chans + chan, EDGE, stride=2 * chans), :].astype(jnp.bfloat16)
                for which in range(2)
            ],
            axis=1,
        )
        slow = dot(w1[...], jnp.concatenate([both, both], axis=0))
        rows = []
        for which in range(2):
            real = slow[:EDGE, which * EDGE : (which + 1) * EDGE]
            imag = slow[EDGE:, which * EDGE : (which + 1) * EDGE]
            rows.append(
                jnp.concatenate([real * cos + imag * sin, imag * cos - real * sin], axis=1)
            )
        high, low = halves(jnp.concatenate(rows, axis=0))
        spectra = dot(high, w2h[...]) + dot(low, w2h[...]) + dot(high, w2l[...])
        ar, ai = spectra[:EDGE, :EDGE], spectra[:EDGE, EDGE:]
        br, bi = spectra[EDGE:, :EDGE], spectra[EDGE:, EDGE:]
        high, low = halves(jnp.concatenate([ar * br - ai * bi, ar * bi + ai * br], axis=1))
        wound = dot(high, w3h[...]) + dot(low, w3h[...]) + dot(high, w3l[...])
        real, imag = wound[:, :EDGE], wound[:, EDGE:]
        high, low = halves(
            jnp.concatenate([real * cos - imag * sin, imag * cos + real * sin], axis=0)
        )
        conv = dot(w4h[...], high) + dot(w4h[...], low) + dot(w4l[...], high)
        back[pl.ds(chan, EDGE, stride=chans), :] = conv

    out_ref[...] = back[...].astype(jnp.bfloat16)


def mix_kernel(conv_ref, value_ref, gate_ref, gate_out_ref, skip_ref, out_ref):
    peers = EDGE // conv_ref.shape[2]
    for part in range(out_ref.shape[1] // EDGE):
        cols = slice(part * EDGE, (part + 1) * EDGE)
        conv = conv_ref[part * peers : (part + 1) * peers, 0].reshape(EDGE, EDGE).T
        gated = (
            gate_ref[:, cols].astype(jnp.float32) * value_ref[:, cols].astype(jnp.float32)
        ).astype(jnp.bfloat16)
        inner = conv.astype(jnp.float32) + skip_ref[:, cols] * gated.astype(jnp.float32)
        out_ref[:, cols] = (gate_out_ref[:, cols].astype(jnp.float32) * inner).astype(
            jnp.bfloat16
        )


def pack(value, gate_in, filt, groups):
    rows, width = value.shape
    chans = width // groups
    block = pl.BlockSpec((EDGE, width), lambda i: (i, 0))
    return pl.pallas_call(
        pack_kernel,
        grid=(rows // EDGE,),
        in_specs=[block] * 3,
        out_specs=pl.BlockSpec((groups, 1, 2, chans, EDGE), lambda i: (0, i, 0, 0, 0)),
        out_shape=jax.ShapeDtypeStruct((groups, rows // EDGE, 2, chans, EDGE), jnp.bfloat16),
        compiler_params=pltpu.CompilerParams(vmem_limit_bytes=VMEM),
        name="pack",
    )(value, gate_in, filt)


def convolve(spread):
    groups, slabs, _, chans, _ = spread.shape
    tables = transform_tables()
    rows = groups * slabs * chans
    whole = pl.BlockSpec(memory_space=pltpu.VMEM)
    conv = pl.pallas_call(
        functools.partial(conv_kernel, chans),
        in_specs=[whole] * (1 + len(tables)),
        out_specs=whole,
        out_shape=jax.ShapeDtypeStruct((rows, EDGE), jnp.bfloat16),
        scratch_shapes=[
            pltpu.VMEM((2 * rows, EDGE), jnp.float32),
            pltpu.VMEM((rows, EDGE), jnp.float32),
        ],
        compiler_params=pltpu.CompilerParams(vmem_limit_bytes=VMEM),
        name="convolve",
    )(spread.reshape(2 * rows, EDGE), *(jnp.asarray(table) for table in tables))
    return conv.reshape(groups, slabs, chans, EDGE)


def mix(conv, value, gate_in, gate_out, skip):
    rows, width = value.shape
    groups, _, chans, _ = conv.shape
    block = pl.BlockSpec((EDGE, width), lambda i: (i, 0))
    return pl.pallas_call(
        mix_kernel,
        grid=(rows // EDGE,),
        in_specs=[
            pl.BlockSpec((groups, 1, chans, EDGE), lambda i: (0, i, 0, 0)),
            block,
            block,
            block,
            pl.BlockSpec((1, width), lambda i: (0, 0)),
        ],
        out_specs=block,
        out_shape=jax.ShapeDtypeStruct((rows, width), jnp.bfloat16),
        compiler_params=pltpu.CompilerParams(vmem_limit_bytes=VMEM),
        name="mix",
    )(conv, value, gate_in, gate_out, skip[None])


def per_device(value, gate_in, gate_out, filt, skip, w_out):
    groups = lax.axis_size("ctx")
    packed = pack(value, gate_in, filt, groups)
    spread = lax.all_to_all(packed, "ctx", split_axis=0, concat_axis=0, tiled=True)
    conv = convolve(spread)
    returned = lax.all_to_all(conv, "ctx", split_axis=0, concat_axis=0, tiled=True)
    mixed = mix(returned, value, gate_in, gate_out, skip)
    partial_out = jnp.dot(mixed, w_out, preferred_element_type=jnp.float32)
    summed = lax.psum_scatter(partial_out, "chan", scatter_dimension=1, tiled=True)
    return summed.astype(jnp.bfloat16)


def solution(mesh):
    placed = (
        P("ctx", "chan"),
        P("ctx", "chan"),
        P("ctx", "chan"),
        P("ctx", "chan"),
        P("chan"),
        P("chan", None),
    )
    return jax.shard_map(
        per_device, mesh=mesh, in_specs=placed, out_specs=P("ctx", "chan"), check_vma=False
    )
```

```python
import functools

import jax
import jax.numpy as jnp
import numpy as np
from jax import lax
from jax.experimental import pallas as pl
from jax.experimental.pallas import tpu as pltpu
from jax.sharding import PartitionSpec as P

EDGE = 128
VMEM = 48 * 1024 * 1024
ALONG_X = 4
CHUNKS = 2
BATCH = 8


def split_table(table):
    high = table.astype(jnp.bfloat16)
    low = (table - high.astype(np.float64)).astype(jnp.bfloat16)
    return high, low


@functools.cache
def transform_tables():
    steps = np.arange(EDGE)
    slow = 2.0 * np.pi * np.outer(steps + 0.25, steps) / EDGE
    fast = 2.0 * np.pi * np.outer(steps, steps) / EDGE
    turn = 2.0 * np.pi * np.outer(steps + 0.25, steps) / (EDGE * EDGE)
    first = np.concatenate([np.cos(slow), -np.sin(slow)], 0)
    second = np.block([[np.cos(fast), -np.sin(fast)], [np.sin(fast), np.cos(fast)]])
    third = np.block([[np.cos(fast), np.sin(fast)], [-np.sin(fast), np.cos(fast)]]) / EDGE
    last = np.concatenate([np.cos(slow).T, -np.sin(slow).T], 1) / EDGE
    first_high, first_low = split_table(first)
    stacked = [np.concatenate([first_high, first_low], 1)]
    for table in (second, third, last):
        stacked.extend(split_table(table))
    return (
        np.concatenate(stacked, 0),
        np.stack([np.cos(turn), np.sin(turn)]).astype(np.float32),
    )


def halves(array):
    high = array.astype(jnp.bfloat16)
    return high, (array - high.astype(jnp.float32)).astype(jnp.bfloat16)


def dot(a, b):
    return jnp.dot(a, b, preferred_element_type=jnp.float32)


def pack_kernel(value_hbm, gate_hbm, filt_hbm, out_ref, held, arrived):
    slabs = out_ref.shape[1]

    def fetch(which, slab):
        array = (value_hbm, gate_hbm, filt_hbm)[which]
        rows = pl.ds(slab * EDGE, EDGE)
        return pltpu.make_async_copy(
            array.at[rows, :], held.at[which, rows, :], arrived.at[which, slab]
        )

    for slab in range(slabs):
        for which in range(3):
            fetch(which, slab).start()
    chans = out_ref.shape[3]
    peers = EDGE // chans
    for slab in range(slabs):
        rows = slice(slab * EDGE, (slab + 1) * EDGE)
        for which in range(3):
            fetch(which, slab).wait()
        gated = held[0, rows].astype(jnp.float32) * held[1, rows].astype(jnp.float32)
        for which, array in enumerate((gated.astype(jnp.bfloat16), held[2, rows])):
            for part in range(array.shape[1] // EDGE):
                turned = array[:, part * EDGE : (part + 1) * EDGE].T
                out_ref[part * peers : (part + 1) * peers, slab, which] = turned.reshape(
                    peers, chans, EDGE
                )


def conv_kernel(chans, in_ref, tables, turns, out_ref, wide, back):
    wide[...] = in_ref[...].astype(jnp.float32)
    cos, sin = turns[0], turns[1]

    def table(index, rows=2 * EDGE):
        start = min(index, 5) * 2 * EDGE + max(index - 5, 0) * EDGE
        return tables[start : start + rows, :]

    def thrice(high, low, index):
        top = table(index)
        return dot(high, top) + dot(low, top) + dot(high, table(index + 1))

    @pl.loop(0, chans // BATCH)
    def _(step):
        first = step * BATCH
        signals = [
            wide[pl.ds(which * chans + first + k, EDGE, stride=2 * chans), :].astype(jnp.bfloat16)
            for k in range(BATCH)
            for which in range(2)
        ]
        both = jnp.concatenate(signals, axis=1)
        slow = dot(table(0), jnp.concatenate([both, both], axis=0))
        rows = []
        for k in range(2 * BATCH):
            cols = slice(k * EDGE, (k + 1) * EDGE)
            real, imag = slow[:EDGE, cols], slow[EDGE:, cols]
            rows.append(
                jnp.concatenate([real * cos + imag * sin, imag * cos - real * sin], axis=1)
            )
        spectra = thrice(*halves(jnp.concatenate(rows, axis=0)), 1)
        rows = []
        for k in range(BATCH):
            ours = spectra[2 * k * EDGE : (2 * k + 1) * EDGE]
            taps = spectra[(2 * k + 1) * EDGE : (2 * k + 2) * EDGE]
            ar, ai, br, bi = ours[:, :EDGE], ours[:, EDGE:], taps[:, :EDGE], taps[:, EDGE:]
            rows.append(jnp.concatenate([ar * br - ai * bi, ar * bi + ai * br], axis=1))
        wound = thrice(*halves(jnp.concatenate(rows, axis=0)), 3)
        cols = []
        for k in range(BATCH):
            real = wound[k * EDGE : (k + 1) * EDGE, :EDGE]
            imag = wound[k * EDGE : (k + 1) * EDGE, EDGE:]
            cols.append(
                jnp.concatenate([real * cos - imag * sin, imag * cos + real * sin], axis=0)
            )
        high, low = halves(jnp.concatenate(cols, axis=1))
        top = table(5, EDGE)
        conv = dot(top, high) + dot(top, low) + dot(table(6, EDGE), high)
        for k in range(BATCH):
            back[pl.ds(first + k, EDGE, stride=chans), :] = conv[:, k * EDGE : (k + 1) * EDGE]

    out_ref[...] = back[...].astype(jnp.bfloat16)


def mix_kernel(_, conv_ref, value_ref, gate_ref, gate_out_ref, skip_ref, out_ref):
    peers = EDGE // conv_ref.shape[2]
    for part in range(out_ref.shape[1] // EDGE):
        cols = slice(part * EDGE, (part + 1) * EDGE)
        conv = conv_ref[part * peers : (part + 1) * peers, 0].reshape(EDGE, EDGE).T
        gated = (
            gate_ref[:, cols].astype(jnp.float32) * value_ref[:, cols].astype(jnp.float32)
        ).astype(jnp.bfloat16)
        inner = conv.astype(jnp.float32) + skip_ref[:, cols] * gated.astype(jnp.float32)
        out_ref[:, cols] = (gate_out_ref[:, cols].astype(jnp.float32) * inner).astype(
            jnp.bfloat16
        )


def deal_kernel(place, w_hbm, own_ref, *rest):
    pieces, done = rest[:-1], rest[-1]
    x, y, core = place[0], place[1], place[2]
    width = own_ref.shape[-1]
    half = width // 2

    def block(row_half, col_half, target):
        col = (lax.rem(y + col_half, 2) * ALONG_X + target) * width
        return w_hbm.at[
            pl.ds(pl.multiple_of(row_half * half, half), half),
            pl.ds(pl.multiple_of(col, width), width),
        ]

    copies = []
    for shift in range(ALONG_X):
        target = lax.rem(x + shift, ALONG_X)
        for col_half in range(2):
            for row_half in range(1 if shift else 2):
                rows = pl.ds(row_half * half, half)
                into = pieces[shift - 1] if shift else own_ref
                copies.append(
                    pltpu.make_async_copy(
                        block(lax.rem(core + row_half, 2), col_half, target),
                        into.at[col_half, rows, :],
                        done.at[len(copies)],
                    )
                )
    for copy in copies:
        copy.start()
    for copy in copies:
        copy.wait()


def project_kernel(col_half, *refs):
    parts, weights, out_ref = refs[:ALONG_X], refs[ALONG_X:-1], refs[-1]
    half = parts[0].shape[1] // 2
    total = dot(parts[0][...], weights[0][col_half])
    for shift in range(1, ALONG_X):
        for row_half in range(2):
            total = total + dot(
                parts[shift][:, row_half * half : (row_half + 1) * half],
                weights[2 * shift - 1 + row_half][col_half],
            )
    out_ref[...] = total.astype(out_ref.dtype)


def pack(value, gate_in, filt, groups):
    rows, width = value.shape
    slabs, chans = rows // EDGE, width // groups
    return pl.pallas_call(
        pack_kernel,
        in_specs=[pl.BlockSpec(memory_space=pl.ANY)] * 3,
        out_specs=pl.BlockSpec(memory_space=pltpu.VMEM),
        out_shape=jax.ShapeDtypeStruct((groups, slabs, 2, chans, EDGE), jnp.bfloat16),
        scratch_shapes=[
            pltpu.VMEM((3, rows, width), jnp.bfloat16),
            pltpu.SemaphoreType.DMA((3, slabs)),
        ],
        compiler_params=pltpu.CompilerParams(vmem_limit_bytes=VMEM),
        name="pack",
    )(value, gate_in, filt)


def convolve(spread):
    groups, slabs, _, chans, _ = spread.shape
    tables = transform_tables()
    rows = groups * slabs * chans
    whole = pl.BlockSpec(memory_space=pltpu.VMEM)
    conv = pl.pallas_call(
        functools.partial(conv_kernel, chans),
        in_specs=[whole] * (1 + len(tables)),
        out_specs=whole,
        out_shape=jax.ShapeDtypeStruct((rows, EDGE), jnp.bfloat16),
        scratch_shapes=[
            pltpu.VMEM((2 * rows, EDGE), jnp.float32),
            pltpu.VMEM((rows, EDGE), jnp.float32),
        ],
        compiler_params=pltpu.CompilerParams(vmem_limit_bytes=VMEM),
        cost_estimate=pl.CostEstimate(
            flops=6 * 10**9, bytes_accessed=2 * 10**6, transcendentals=0
        ),
        name="convolve",
    )(spread.reshape(2 * rows, EDGE), *(jnp.asarray(table) for table in tables))
    return conv.reshape(groups, slabs, chans, EDGE)


def mix(conv, value, gate_in, gate_out, skip, core):
    rows, width = value.shape
    groups, _, chans, _ = conv.shape
    block = pl.BlockSpec((EDGE, width // 2), lambda i, j, core: (i, j))
    return pl.pallas_call(
        mix_kernel,
        grid_spec=pltpu.PrefetchScalarGridSpec(
            num_scalar_prefetch=1,
            grid=(rows // EDGE, 2),
            in_specs=[
                pl.BlockSpec((groups // 2, 1, chans, EDGE), lambda i, j, core: (j, i, 0, 0)),
                block,
                block,
                block,
                pl.BlockSpec((1, width // 2), lambda i, j, core: (0, j)),
            ],
            out_specs=pl.BlockSpec(
                (EDGE, width // 2), lambda i, j, core: (i, lax.rem(j + core[0], 2))
            ),
        ),
        out_shape=jax.ShapeDtypeStruct((rows, width), jnp.bfloat16),
        compiler_params=pltpu.CompilerParams(vmem_limit_bytes=VMEM),
        name="mix",
    )(core, conv, value, gate_in, gate_out, skip[None])


def deal(w_out, place, width):
    whole = pl.BlockSpec(memory_space=pltpu.VMEM)
    shapes = [(2, width, width)] + [(2, width // 2, width)] * (ALONG_X - 1)
    return pl.pallas_call(
        deal_kernel,
        in_specs=[
            pl.BlockSpec(memory_space=pltpu.SMEM),
            pl.BlockSpec(memory_space=pl.ANY),
        ],
        out_specs=[whole] * ALONG_X,
        out_shape=[jax.ShapeDtypeStruct(shape, jnp.bfloat16) for shape in shapes],
        scratch_shapes=[pltpu.SemaphoreType.DMA((2 * ALONG_X + 2,))],
        compiler_params=pltpu.CompilerParams(vmem_limit_bytes=VMEM),
        name="deal",
    )(place, w_out)


def project_half(parts, weights, col_half, dtype):
    rows, width = parts[0].shape
    whole = pl.BlockSpec(memory_space=pltpu.VMEM)
    return pl.pallas_call(
        functools.partial(project_kernel, col_half),
        in_specs=[whole] * (len(parts) + len(weights)),
        out_specs=whole,
        out_shape=jax.ShapeDtypeStruct((rows, width), dtype),
        compiler_params=pltpu.CompilerParams(vmem_limit_bytes=VMEM),
        cost_estimate=pl.CostEstimate(
            flops=2 * rows * ALONG_X * width * width, bytes_accessed=3 * 10**6, transcendentals=0
        ),
        name="project",
    )(*parts, *weights)


def along_x(shift):
    return [
        (i, i // ALONG_X * ALONG_X + (i + shift) % ALONG_X) for i in range(2 * ALONG_X)
    ]


def across_y():
    return [(i, (i + ALONG_X) % (2 * ALONG_X)) for i in range(2 * ALONG_X)]


def project(mixed, weights):
    rows, width = mixed.shape
    depth = rows // CHUNKS
    parts, theirs, outs = [], [], []
    for chunk in range(CHUNKS):
        own = mixed[chunk * depth : (chunk + 1) * depth]
        parts.append(
            [own]
            + [lax.ppermute(own, "chan", along_x(shift)) for shift in range(1, ALONG_X)]
        )
    for chunk in range(CHUNKS):
        share = project_half(parts[chunk], weights, 1, jnp.bfloat16)
        theirs.append(lax.ppermute(share, "chan", across_y()))
    for chunk in range(CHUNKS):
        mine = project_half(parts[chunk], weights, 0, jnp.float32)
        outs.append((mine + theirs[chunk].astype(jnp.float32)).astype(jnp.bfloat16))
    return jnp.concatenate(outs, axis=0)


def per_device(value, gate_in, gate_out, filt, skip, w_out):
    groups = lax.axis_size("ctx")
    place = lax.axis_index("chan")
    core = lax.rem(lax.axis_index("ctx"), 2)
    where = jnp.stack([lax.rem(place, ALONG_X), lax.div(place, ALONG_X), core])
    own, *pieces = deal(w_out, where, value.shape[1])
    pieces = [lax.ppermute(piece, "chan", along_x(i + 1)) for i, piece in enumerate(pieces)]
    packed = pack(value, gate_in, filt, groups)
    spread = lax.all_to_all(packed, "ctx", split_axis=0, concat_axis=0, tiled=True)
    spread, *pieces = lax.optimization_barrier((spread, *pieces))
    other = [(i, i ^ 1) for i in range(groups)]
    halves_of_core = [lax.ppermute(piece, "ctx", other) for piece in pieces]
    conv = convolve(spread)
    conv, *halves_of_core = lax.optimization_barrier((conv, *halves_of_core))
    returned = lax.all_to_all(conv, "ctx", split_axis=0, concat_axis=0, tiled=True)
    mixed = mix(returned, value, gate_in, gate_out, skip, core[None])
    weights = [own]
    for ours, theirs in zip(pieces, halves_of_core):
        weights += [ours, theirs]
    return project(mixed, weights)


def solution(mesh):
    placed = (
        P("ctx", "chan"),
        P("ctx", "chan"),
        P("ctx", "chan"),
        P("ctx", "chan"),
        P("chan"),
        P("chan", None),
    )
    return jax.shard_map(
        per_device, mesh=mesh, in_specs=placed, out_specs=P("ctx", "chan"), check_vma=False
    )
```

```python
import functools

import jax
import jax.numpy as jnp
import numpy as np
from jax import lax
from jax.experimental import pallas as pl
from jax.experimental.pallas import tpu as pltpu
from jax.sharding import PartitionSpec as P

EDGE = 128
WIDE = 48 * 1024 * 1024
ALONG_X = 4
FIRST_SLABS = 2
BATCH = 8


def split_table(table):
    high = table.astype(jnp.bfloat16)
    low = (table - high.astype(np.float64)).astype(jnp.bfloat16)
    return high, low


@functools.cache
def transform_tables():
    steps = np.arange(EDGE)
    slow = 2.0 * np.pi * np.outer(steps + 0.25, steps) / EDGE
    fast = 2.0 * np.pi * np.outer(steps, steps) / EDGE
    turn = 2.0 * np.pi * np.outer(steps + 0.25, steps) / (EDGE * EDGE)
    first = np.concatenate([np.cos(slow), -np.sin(slow)], 0)
    second = np.block([[np.cos(fast), -np.sin(fast)], [np.sin(fast), np.cos(fast)]])
    third = np.block([[np.cos(fast), np.sin(fast)], [-np.sin(fast), np.cos(fast)]]) / EDGE
    last = np.concatenate([np.cos(slow).T, -np.sin(slow).T], 1) / EDGE
    first_high, first_low = split_table(first)
    stacked = [np.concatenate([first_high, first_low], 1)]
    for table in (second, third):
        stacked.extend(split_table(table))
    return (
        np.concatenate(stacked, 0),
        np.concatenate(split_table(last), 1),
        np.stack([np.cos(turn), np.sin(turn)]).astype(np.float32),
    )


def thirds(array, axis):
    high = array.astype(jnp.bfloat16)
    low = (array - high.astype(jnp.float32)).astype(jnp.bfloat16)
    return jnp.concatenate([high, low, high], axis=axis)


def dot(a, b):
    return jnp.dot(a, b, preferred_element_type=jnp.float32)


def pack_kernel(value_hbm, gate_hbm, filt_hbm, out_ref, held, arrived):
    slabs, _, chans, _ = out_ref.shape[1:]
    arrays = (value_hbm, gate_hbm, filt_hbm)

    def fetch(which, slab):
        rows = pl.ds(slab * EDGE, EDGE)
        return pltpu.make_async_copy(
            arrays[which].at[rows, :], held.at[which, rows, :], arrived.at[which, slab]
        )

    for slab in range(slabs):
        for which in range(3):
            fetch(which, slab).start()
    peers = EDGE // chans
    for slab in range(slabs):
        rows = slice(slab * EDGE, (slab + 1) * EDGE)
        for which in range(3):
            fetch(which, slab).wait()
        gated = held[0, rows].astype(jnp.float32) * held[1, rows].astype(jnp.float32)
        gated = gated.astype(jnp.bfloat16)
        for which, array in enumerate((gated, held[2, rows])):
            for part in range(array.shape[1] // EDGE):
                turned = array[:, part * EDGE : (part + 1) * EDGE].T
                out_ref[part * peers : (part + 1) * peers, slab, which] = turned.reshape(
                    peers, chans, EDGE
                )


def copy_all(copies):
    for copy in copies:
        copy.start()
    for copy in copies:
        copy.wait()


def deal_kernel(place, w_hbm, *rest):
    pieces, done = rest[:-1], rest[-1]
    copies = []
    for i, piece in enumerate(pieces):
        _, height, width = piece.shape
        target = lax.rem(place[0] + i + 1, ALONG_X)
        for side in range(2):
            col = (lax.rem(place[1] + side, 2) * ALONG_X + target) * width
            block = w_hbm.at[:, pl.ds(pl.multiple_of(col, width), width)]
            copies.append(pltpu.make_async_copy(block, piece.at[side], done.at[i, side]))
    for copy in copies:
        copy.start()
    for copy in copies:
        copy.wait()


def conv_kernel(chans, in_ref, tables, last, turns, out_ref, wide, back):
    wide[...] = in_ref[...].astype(jnp.float32)
    cos, sin = turns[0], turns[1]

    def three(index):
        high = tables[2 * EDGE * index : 2 * EDGE * (index + 1), :]
        low = tables[2 * EDGE * (index + 1) : 2 * EDGE * (index + 2), :]
        return jnp.concatenate([high, high, low], axis=0)

    def last_three():
        high, low = last[:, : 2 * EDGE], last[:, 2 * EDGE :]
        return jnp.concatenate([high, high, low], axis=1)


    @pl.loop(0, chans // BATCH)
    def _(step):
        first = step * BATCH
        signals = [
            wide[pl.ds(which * chans + first + k, EDGE, stride=2 * chans), :].astype(jnp.bfloat16)
            for k in range(BATCH)
            for which in range(2)
        ]
        both = jnp.concatenate(signals, axis=1)
        slow = dot(tables[: 2 * EDGE, :], jnp.concatenate([both, both], axis=0))
        rows = []
        for k in range(2 * BATCH):
            cols = slice(k * EDGE, (k + 1) * EDGE)
            real, imag = slow[:EDGE, cols], slow[EDGE:, cols]
            rows.append(
                jnp.concatenate([real * cos + imag * sin, imag * cos - real * sin], axis=1)
            )
        spectra = dot(thirds(jnp.concatenate(rows, axis=0), 1), three(1))
        rows = []
        for k in range(BATCH):
            ours = spectra[2 * k * EDGE : (2 * k + 1) * EDGE]
            taps = spectra[(2 * k + 1) * EDGE : (2 * k + 2) * EDGE]
            ar, ai, br, bi = ours[:, :EDGE], ours[:, EDGE:], taps[:, :EDGE], taps[:, EDGE:]
            rows.append(jnp.concatenate([ar * br - ai * bi, ar * bi + ai * br], axis=1))
        wound = dot(thirds(jnp.concatenate(rows, axis=0), 1), three(3))
        cols = []
        for k in range(BATCH):
            real = wound[k * EDGE : (k + 1) * EDGE, :EDGE]
            imag = wound[k * EDGE : (k + 1) * EDGE, EDGE:]
            cols.append(
                jnp.concatenate([real * cos - imag * sin, imag * cos + real * sin], axis=0)
            )
        conv = dot(last_three(), thirds(jnp.concatenate(cols, axis=1), 0))
        for k in range(BATCH):
            back[pl.ds(first + k, EDGE, stride=chans), :] = conv[:, k * EDGE : (k + 1) * EDGE]

    out_ref[...] = back[...].astype(jnp.bfloat16)


def mix_kernel(conv_ref, value_ref, gate_ref, gate_out_ref, skip_ref, *outs):
    slabs, chans = conv_ref.shape[1:3]
    width = value_ref.shape[1]
    peers = EDGE // chans
    for slab in range(slabs):
        rows = slice(slab * EDGE, (slab + 1) * EDGE)
        out_ref, first = outs[0], slab
        if slab >= FIRST_SLABS:
            out_ref, first = outs[1], slab - FIRST_SLABS
        out_rows = slice(first * EDGE, (first + 1) * EDGE)
        for part in range(width // EDGE):
            cols = slice(part * EDGE, (part + 1) * EDGE)
            conv = conv_ref[part * peers : (part + 1) * peers, slab].reshape(EDGE, EDGE).T
            gated = gate_ref[rows, cols].astype(jnp.float32) * value_ref[rows, cols].astype(
                jnp.float32
            )
            gated = gated.astype(jnp.bfloat16).astype(jnp.float32)
            inner = conv.astype(jnp.float32) + skip_ref[:, cols] * gated
            mixed = gate_out_ref[rows, cols].astype(jnp.float32) * inner
            out_ref[out_rows, cols] = mixed.astype(jnp.bfloat16)


def project_kernel(n_parts, *refs):
    parts, weights, out_ref = refs[:n_parts], refs[n_parts:-1], refs[-1]

    def product(part, shift):
        return dot(part[...], weights[shift][0])

    total = product(parts[0], 0) + product(parts[1], 1) + product(parts[-1], ALONG_X - 1)
    across = jnp.concatenate([product(part, 2) for part in parts[2:-1]], axis=0)
    out_ref[...] = (total + across).astype(out_ref.dtype)


def pack(value, gate_in, filt, groups):
    rows, width = value.shape
    slabs, chans = rows // EDGE, width // groups
    return pl.pallas_call(
        pack_kernel,
        in_specs=[pl.BlockSpec(memory_space=pl.ANY)] * 3,
        out_specs=pl.BlockSpec(memory_space=pltpu.VMEM),
        out_shape=jax.ShapeDtypeStruct((groups, slabs, 2, chans, EDGE), jnp.bfloat16),
        scratch_shapes=[
            pltpu.VMEM((3, rows, width), jnp.bfloat16),
            pltpu.SemaphoreType.DMA((3, slabs)),
        ],
        name="pack",
    )(value, gate_in, filt)


def deal(w_out, place, width):
    shape = jax.ShapeDtypeStruct((2, w_out.shape[0], width), jnp.bfloat16)
    return pl.pallas_call(
        deal_kernel,
        in_specs=[pl.BlockSpec(memory_space=pltpu.SMEM), pl.BlockSpec(memory_space=pl.ANY)],
        out_specs=[pl.BlockSpec(memory_space=pltpu.VMEM)] * ALONG_X,
        out_shape=[shape] * ALONG_X,
        scratch_shapes=[pltpu.SemaphoreType.DMA((ALONG_X, 2))],
        compiler_params=pltpu.CompilerParams(vmem_limit_bytes=WIDE),
        name="deal",
    )(place, w_out)


def convolve(spread, tables):
    groups, slabs, _, chans, _ = spread.shape
    rows = groups * slabs * chans
    whole = pl.BlockSpec(memory_space=pltpu.VMEM)
    conv = pl.pallas_call(
        functools.partial(conv_kernel, chans),
        in_specs=[whole] * (1 + len(tables)),
        out_specs=whole,
        out_shape=jax.ShapeDtypeStruct((rows, EDGE), jnp.bfloat16),
        scratch_shapes=[
            pltpu.VMEM((2 * rows, EDGE), jnp.float32),
            pltpu.VMEM((rows, EDGE), jnp.float32),
        ],
        compiler_params=pltpu.CompilerParams(vmem_limit_bytes=WIDE),
        cost_estimate=pl.CostEstimate(
            flops=6 * 10**9, bytes_accessed=2 * 10**6, transcendentals=0
        ),
        name="convolve",
    )(spread.reshape(2 * rows, EDGE), *tables)
    return conv.reshape(groups, slabs, chans, EDGE)


def mix(conv, value, gate_in, gate_out, skip):
    rows, width = value.shape
    first = FIRST_SLABS * EDGE
    whole = pl.BlockSpec(memory_space=pltpu.VMEM)
    return pl.pallas_call(
        mix_kernel,
        in_specs=[whole] * 5,
        out_specs=[whole] * 2,
        out_shape=[
            jax.ShapeDtypeStruct((count, width), jnp.bfloat16) for count in (first, rows - first)
        ],
        compiler_params=pltpu.CompilerParams(vmem_limit_bytes=WIDE),
        name="mix",
    )(conv, value, gate_in, gate_out, skip)


def project_half(parts, weights, side, dtype):
    rows, width = parts[0].shape
    return pl.pallas_call(
        functools.partial(project_kernel, len(parts)),
        grid=(1,),
        in_specs=[pl.BlockSpec(part.shape, lambda i: (0, 0)) for part in parts]
        + [pl.BlockSpec((1, *weight.shape[1:]), lambda i: (side, 0, 0)) for weight in weights],
        out_specs=pl.BlockSpec((rows, width), lambda i: (0, 0)),
        out_shape=jax.ShapeDtypeStruct((rows, width), dtype),
        compiler_params=pltpu.CompilerParams(vmem_limit_bytes=WIDE),
        cost_estimate=pl.CostEstimate(
            flops=2 * rows * ALONG_X * width * width, bytes_accessed=3 * 10**6, transcendentals=0
        ),
        name="project",
    )(*parts, *weights)


def along_x(shift):
    return [
        (i, i // ALONG_X * ALONG_X + (i + shift) % ALONG_X) for i in range(2 * ALONG_X)
    ]


def across_y():
    return [(i, (i + ALONG_X) % (2 * ALONG_X)) for i in range(2 * ALONG_X)]


def gather_x(own):
    def send(rows, shift):
        return lax.ppermute(rows, "chan", along_x(shift))

    before, after = send(own, 1), send(own, ALONG_X - 1)
    half = own.shape[0] // 2
    return [own, before, send(before[:half], 1), send(after[half:], ALONG_X - 1), after]


def per_device(value, gate_in, gate_out, filt, skip, w_out):
    groups = lax.axis_size("ctx")
    place = lax.axis_index("chan")
    where = jnp.stack([lax.rem(place, ALONG_X), lax.div(place, ALONG_X)])
    packed = pack(value, gate_in, filt, groups)
    *pieces, own = deal(w_out, where, value.shape[1])
    pieces = [lax.ppermute(piece, "chan", along_x(i + 1)) for i, piece in enumerate(pieces)]
    spread = lax.all_to_all(packed, "ctx", split_axis=0, concat_axis=0, tiled=True)
    tables = [jnp.asarray(table) for table in transform_tables()]
    conv = convolve(spread, tables)
    returned = lax.all_to_all(conv, "ctx", split_axis=0, concat_axis=0, tiled=True)
    mixed = mix(returned, value, gate_in, gate_out, skip[None])
    mixed, pieces = lax.optimization_barrier((mixed, pieces))
    weights = [own, *pieces]
    parts = [gather_x(rows) for rows in mixed]
    theirs, outs = [], []
    for part in parts:
        share = project_half(part, weights, 1, jnp.bfloat16)
        theirs.append(lax.ppermute(share, "chan", across_y()))
    for part, arrived in zip(parts, theirs):
        mine = project_half(part, weights, 0, jnp.float32)
        outs.append((mine + arrived.astype(jnp.float32)).astype(jnp.bfloat16))
    return jnp.concatenate(outs, axis=0)


def solution(mesh):
    placed = (
        P("ctx", "chan"),
        P("ctx", "chan"),
        P("ctx", "chan"),
        P("ctx", "chan"),
        P("chan"),
        P("chan", None),
    )
    return jax.shard_map(
        per_device, mesh=mesh, in_specs=placed, out_specs=P("ctx", "chan"), check_vma=False
    )
```

```python
import functools

import jax
import jax.numpy as jnp
import numpy as np
from jax import lax
from jax.experimental import pallas as pl
from jax.experimental.pallas import tpu as pltpu
from jax.sharding import PartitionSpec as P

EDGE = 128
WIDE = 48 * 1024 * 1024
MEDIUM = 32 * 1024 * 1024
SMALL = 16 * 1024 * 1024
ALONG_X = 4
RUNS = (2, 2)
BATCH = 8


def split_table(table):
    high = table.astype(jnp.bfloat16)
    low = (table - high.astype(np.float64)).astype(jnp.bfloat16)
    return high, low


@functools.cache
def transform_tables():
    steps = np.arange(EDGE)
    slow = 2.0 * np.pi * np.outer(steps + 0.25, steps) / EDGE
    fast = 2.0 * np.pi * np.outer(steps, steps) / EDGE
    turn = 2.0 * np.pi * np.outer(steps + 0.25, steps) / (EDGE * EDGE)
    first = np.concatenate([np.cos(slow), -np.sin(slow)], 0)
    second = np.concatenate([np.cos(fast), np.sin(fast)], 1)
    return (
        np.concatenate(split_table(first), 1),
        np.concatenate(split_table(second), 1),
        np.stack([np.cos(turn), np.sin(turn)]).astype(np.float32),
    )


def build_tables(first, base, second, third, last):
    for part in range(2):
        cos = base[:, 2 * part * EDGE : (2 * part + 1) * EDGE]
        sin = base[:, (2 * part + 1) * EDGE : (2 * part + 2) * EDGE]
        ahead = jnp.concatenate(
            [jnp.concatenate([cos, -sin], axis=1), jnp.concatenate([sin, cos], axis=1)], axis=0
        )
        back = jnp.concatenate(
            [jnp.concatenate([cos, sin], axis=1), jnp.concatenate([-sin, cos], axis=1)], axis=0
        )
        end = jnp.concatenate(
            [
                first[half * EDGE : (half + 1) * EDGE, part * EDGE : (part + 1) * EDGE].T
                for half in range(2)
            ],
            axis=1,
        )
        scale = jnp.bfloat16(1.0 / EDGE)
        for place in ((0, 1), (2,))[part]:
            rows = slice(2 * place * EDGE, 2 * (place + 1) * EDGE)
            second[rows, :] = ahead
            third[rows, :] = back * scale
            last[:, rows] = end * scale


def thirds(array, axis):
    high = array.astype(jnp.bfloat16)
    low = (array - high.astype(jnp.float32)).astype(jnp.bfloat16)
    return jnp.concatenate([high, low, high], axis=axis)


def dot(a, b):
    return jnp.dot(a, b, preferred_element_type=jnp.float32)


def pack_kernel(value_hbm, gate_hbm, filt_hbm, out_ref, held, arrived):
    slabs, _, chans, _ = out_ref.shape[1:]
    arrays = (value_hbm, gate_hbm, filt_hbm)

    def fetch(which, slab):
        rows = pl.ds(slab * EDGE, EDGE)
        return pltpu.make_async_copy(
            arrays[which].at[rows, :], held.at[which, rows, :], arrived.at[which, slab]
        )

    for slab in range(slabs):
        for which in range(3):
            fetch(which, slab).start()
    peers = EDGE // chans
    for slab in range(slabs):
        rows = slice(slab * EDGE, (slab + 1) * EDGE)
        for which in range(3):
            fetch(which, slab).wait()
        gated = held[0, rows].astype(jnp.float32) * held[1, rows].astype(jnp.float32)
        gated = gated.astype(jnp.bfloat16)
        for which, array in enumerate((gated, held[2, rows])):
            for part in range(array.shape[1] // EDGE):
                turned = array[:, part * EDGE : (part + 1) * EDGE].T
                out_ref[part * peers : (part + 1) * peers, slab, which] = turned.reshape(
                    peers, chans, EDGE
                )


def copy_all(copies):
    for copy in copies:
        copy.start()
    for copy in copies:
        copy.wait()


def deal_kernel(place, w_hbm, *rest):
    pieces, done = rest[:-1], rest[-1]
    copies = []
    for i, piece in enumerate(pieces):
        _, height, width = piece.shape
        target = lax.rem(place[0] + i + 1, ALONG_X)
        for side in range(2):
            col = (lax.rem(place[1] + side, 2) * ALONG_X + target) * width
            block = w_hbm.at[:, pl.ds(pl.multiple_of(col, width), width)]
            copies.append(pltpu.make_async_copy(block, piece.at[side], done.at[i, side]))
    for copy in copies:
        copy.start()
    for copy in copies:
        copy.wait()


def conv_kernel(
    chans, in_ref, first_table, base, turns, out_ref, wide, back, second, third, last
):
    build_tables(first_table, base, second, third, last)
    wide[...] = in_ref[...].astype(jnp.float32)
    cos, sin = turns[0], turns[1]

    @pl.loop(0, chans // BATCH, unroll=True)
    def _(step):
        first = step * BATCH
        signals = [
            wide[pl.ds(which * chans + first + k, EDGE, stride=2 * chans), :].astype(jnp.bfloat16)
            for k in range(BATCH)
            for which in range(2)
        ]
        both = jnp.concatenate(signals, axis=1)
        slow = dot(first_table[...], jnp.concatenate([both, both], axis=0))
        rows = []
        for k in range(2 * BATCH):
            cols = slice(k * EDGE, (k + 1) * EDGE)
            real, imag = slow[:EDGE, cols], slow[EDGE:, cols]
            rows.append(
                jnp.concatenate([real * cos + imag * sin, imag * cos - real * sin], axis=1)
            )
        spectra = dot(thirds(jnp.concatenate(rows, axis=0), 1), second[...])
        rows = []
        for k in range(BATCH):
            ours = spectra[2 * k * EDGE : (2 * k + 1) * EDGE]
            taps = spectra[(2 * k + 1) * EDGE : (2 * k + 2) * EDGE]
            ar, ai, br, bi = ours[:, :EDGE], ours[:, EDGE:], taps[:, :EDGE], taps[:, EDGE:]
            rows.append(jnp.concatenate([ar * br - ai * bi, ar * bi + ai * br], axis=1))
        wound = dot(thirds(jnp.concatenate(rows, axis=0), 1), third[...])
        cols = []
        for k in range(BATCH):
            real = wound[k * EDGE : (k + 1) * EDGE, :EDGE]
            imag = wound[k * EDGE : (k + 1) * EDGE, EDGE:]
            cols.append(
                jnp.concatenate([real * cos - imag * sin, imag * cos + real * sin], axis=0)
            )
        conv = dot(last[...], thirds(jnp.concatenate(cols, axis=1), 0))
        for k in range(BATCH):
            back[pl.ds(first + k, EDGE, stride=chans), :] = conv[:, k * EDGE : (k + 1) * EDGE]

    out_ref[...] = back[...].astype(jnp.bfloat16)


def mix_kernel(conv_ref, value_ref, gate_ref, gate_out_ref, skip_ref, *outs):
    slabs, chans = conv_ref.shape[1:3]
    width = value_ref.shape[1]
    peers = EDGE // chans
    for slab in range(slabs):
        rows = slice(slab * EDGE, (slab + 1) * EDGE)
        run, first = [(run, k) for run, count in enumerate(RUNS) for k in range(count)][slab]
        out_rows = slice(first * EDGE, (first + 1) * EDGE)
        for part in range(width // EDGE):
            cols = slice(part * EDGE, (part + 1) * EDGE)
            conv = conv_ref[part * peers : (part + 1) * peers, slab].reshape(EDGE, EDGE).T
            gated = gate_ref[rows, cols].astype(jnp.float32) * value_ref[rows, cols].astype(
                jnp.float32
            )
            gated = gated.astype(jnp.bfloat16).astype(jnp.float32)
            inner = conv.astype(jnp.float32) + skip_ref[:, cols] * gated
            mixed = gate_out_ref[rows, cols].astype(jnp.float32) * inner
            outs[run][out_rows, cols] = mixed.astype(jnp.bfloat16)


def project_kernel(*refs):
    *parts, weights, out_ref = refs

    def product(part, shift):
        return dot(part[...], weights[shift])

    total = product(parts[0], 0) + product(parts[1], 1) + product(parts[-1], ALONG_X - 1)
    across = jnp.concatenate([product(part, 2) for part in parts[2:-1]], axis=0)
    out_ref[...] = (total + across).astype(out_ref.dtype)


def pack(value, gate_in, filt, groups):
    rows, width = value.shape
    slabs, chans = rows // EDGE, width // groups
    return pl.pallas_call(
        pack_kernel,
        in_specs=[pl.BlockSpec(memory_space=pl.ANY)] * 3,
        out_specs=pl.BlockSpec(memory_space=pltpu.VMEM),
        out_shape=jax.ShapeDtypeStruct((groups, slabs, 2, chans, EDGE), jnp.bfloat16),
        scratch_shapes=[
            pltpu.VMEM((3, rows, width), jnp.bfloat16),
            pltpu.SemaphoreType.DMA((3, slabs)),
        ],
        name="pack",
    )(value, gate_in, filt)


def deal(w_out, place, width):
    shape = jax.ShapeDtypeStruct((2, w_out.shape[0], width), jnp.bfloat16)
    return pl.pallas_call(
        deal_kernel,
        in_specs=[pl.BlockSpec(memory_space=pltpu.SMEM), pl.BlockSpec(memory_space=pl.ANY)],
        out_specs=[pl.BlockSpec(memory_space=pltpu.VMEM)] * ALONG_X,
        out_shape=[shape] * ALONG_X,
        scratch_shapes=[pltpu.SemaphoreType.DMA((ALONG_X, 2))],
        compiler_params=pltpu.CompilerParams(vmem_limit_bytes=WIDE),
        name="deal",
    )(place, w_out)


def convolve(spread, tables):
    groups, slabs, _, chans, _ = spread.shape
    rows = groups * slabs * chans
    whole = pl.BlockSpec(memory_space=pltpu.VMEM)
    conv = pl.pallas_call(
        functools.partial(conv_kernel, chans),
        in_specs=[whole] * (1 + len(tables)),
        out_specs=whole,
        out_shape=jax.ShapeDtypeStruct((rows, EDGE), jnp.bfloat16),
        scratch_shapes=[
            pltpu.VMEM((2 * rows, EDGE), jnp.float32),
            pltpu.VMEM((rows, EDGE), jnp.float32),
            pltpu.VMEM((6 * EDGE, 2 * EDGE), jnp.bfloat16),
            pltpu.VMEM((6 * EDGE, 2 * EDGE), jnp.bfloat16),
            pltpu.VMEM((EDGE, 6 * EDGE), jnp.bfloat16),
        ],
        compiler_params=pltpu.CompilerParams(vmem_limit_bytes=MEDIUM),
        cost_estimate=pl.CostEstimate(
            flops=6 * 10**9, bytes_accessed=2 * 10**6, transcendentals=0
        ),
        name="convolve",
    )(spread.reshape(2 * rows, EDGE), *tables)
    return conv.reshape(groups, slabs, chans, EDGE)


def mix(conv, value, gate_in, gate_out, skip):
    width = value.shape[1]
    whole = pl.BlockSpec(memory_space=pltpu.VMEM)
    return pl.pallas_call(
        mix_kernel,
        in_specs=[whole] * 5,
        out_specs=[whole] * len(RUNS),
        out_shape=[jax.ShapeDtypeStruct((run * EDGE, width), jnp.bfloat16) for run in RUNS],
        compiler_params=pltpu.CompilerParams(vmem_limit_bytes=SMALL),
        name="mix",
    )(conv, value, gate_in, gate_out, skip)


def stage_kernel(side, *refs):
    weights, out_ref, done = refs[:-2], refs[-2], refs[-1]
    copies = [
        pltpu.make_async_copy(weight.at[side], out_ref.at[shift], done.at[shift])
        for shift, weight in enumerate(weights)
    ]
    for copy in copies:
        copy.start()
    for copy in copies:
        copy.wait()


def stage(weights, side):
    return pl.pallas_call(
        functools.partial(stage_kernel, side),
        in_specs=[pl.BlockSpec(memory_space=pl.ANY)] * len(weights),
        out_specs=pl.BlockSpec(memory_space=pltpu.VMEM),
        out_shape=jax.ShapeDtypeStruct((len(weights), *weights[0].shape[1:]), jnp.bfloat16),
        scratch_shapes=[pltpu.SemaphoreType.DMA((len(weights),))],
        compiler_params=pltpu.CompilerParams(vmem_limit_bytes=SMALL),
        cost_estimate=pl.CostEstimate(flops=0, bytes_accessed=8 * 10**6, transcendentals=0),
        name="stage",
    )(*weights)


def project_half(parts, weights, dtype):
    rows, width = parts[0].shape
    whole = pl.BlockSpec(memory_space=pltpu.VMEM)
    return pl.pallas_call(
        project_kernel,
        in_specs=[whole] * (len(parts) + 1),
        out_specs=whole,
        out_shape=jax.ShapeDtypeStruct((rows, width), dtype),
        compiler_params=pltpu.CompilerParams(vmem_limit_bytes=SMALL),
        cost_estimate=pl.CostEstimate(
            flops=2 * rows * ALONG_X * width * width, bytes_accessed=3 * 10**6, transcendentals=0
        ),
        name="project",
    )(*parts, weights)


def along_x(shift):
    return [
        (i, i // ALONG_X * ALONG_X + (i + shift) % ALONG_X) for i in range(2 * ALONG_X)
    ]


def across_y():
    return [(i, (i + ALONG_X) % (2 * ALONG_X)) for i in range(2 * ALONG_X)]


def gather_x(own):
    def send(rows, shift):
        return lax.ppermute(rows, "chan", along_x(shift))

    before, after = send(own, 1), send(own, ALONG_X - 1)
    half = own.shape[0] // 2
    return [own, before, send(before[:half], 1), send(after[half:], ALONG_X - 1), after]


def per_device(value, gate_in, gate_out, filt, skip, w_out):
    groups = lax.axis_size("ctx")
    place = lax.axis_index("chan")
    where = jnp.stack([lax.rem(place, ALONG_X), lax.div(place, ALONG_X)])
    packed = pack(value, gate_in, filt, groups)
    *pieces, own = deal(w_out, where, value.shape[1])
    pieces = [lax.ppermute(piece, "chan", along_x(i + 1)) for i, piece in enumerate(pieces)]
    spread = lax.all_to_all(packed, "ctx", split_axis=0, concat_axis=0, tiled=True)
    tables = [jnp.asarray(table) for table in transform_tables()]
    conv = convolve(spread, tables)
    returned = lax.all_to_all(conv, "ctx", split_axis=0, concat_axis=0, tiled=True)
    mixed = mix(returned, value, gate_in, gate_out, skip[None])
    mixed, pieces = lax.optimization_barrier((mixed, pieces))
    parts = [gather_x(rows) for rows in mixed]
    weights = [own, *pieces]
    outs = []
    staged = stage(weights, 1)
    shares = [project_half(part, staged, jnp.bfloat16) for part in parts]
    theirs = [lax.ppermute(share, "chan", across_y()) for share in shares]
    weights, _ = lax.optimization_barrier((weights, shares))
    staged = stage(weights, 0)
    for part, arrived in zip(parts, theirs):
        mine = project_half(part, staged, jnp.float32)
        outs.append((mine + arrived.astype(jnp.float32)).astype(jnp.bfloat16))
    return jnp.concatenate(outs, axis=0)


def solution(mesh):
    placed = (
        P("ctx", "chan"),
        P("ctx", "chan"),
        P("ctx", "chan"),
        P("ctx", "chan"),
        P("chan"),
        P("chan", None),
    )
    return jax.shard_map(
        per_device, mesh=mesh, in_specs=placed, out_specs=P("ctx", "chan"), check_vma=False
    )
```

```python
import functools

import jax
import jax.numpy as jnp
import numpy as np
from jax import lax
from jax.experimental import pallas as pl
from jax.experimental.pallas import tpu as pltpu
from jax.sharding import PartitionSpec as P

EDGE = 128
WIDE = 48 * 1024 * 1024
MEDIUM = 32 * 1024 * 1024
SMALL = 16 * 1024 * 1024
ALONG_X = 4
RUNS = (2, 2)
BATCH = 8


def split_table(table):
    high = table.astype(jnp.bfloat16)
    low = (table - high.astype(np.float64)).astype(jnp.bfloat16)
    return high, low


@functools.cache
def transform_tables():
    steps = np.arange(EDGE)
    slow = 2.0 * np.pi * np.outer(steps + 0.25, steps) / EDGE
    fast = 2.0 * np.pi * np.outer(steps, steps) / EDGE
    turn = 2.0 * np.pi * np.outer(steps + 0.25, steps) / (EDGE * EDGE)
    first = np.concatenate([np.cos(slow), -np.sin(slow)], 0)
    second = np.concatenate([np.cos(fast), np.sin(fast)], 1)
    return (
        np.concatenate(split_table(first), 1),
        np.concatenate(split_table(second), 1),
        np.stack([np.cos(turn), np.sin(turn)]).astype(np.float32),
    )


def build_tables(first, base, second, third, last):
    for part in range(2):
        cos = base[:, 2 * part * EDGE : (2 * part + 1) * EDGE]
        sin = base[:, (2 * part + 1) * EDGE : (2 * part + 2) * EDGE]
        ahead = jnp.concatenate(
            [jnp.concatenate([cos, -sin], axis=1), jnp.concatenate([sin, cos], axis=1)], axis=0
        )
        back = jnp.concatenate(
            [jnp.concatenate([cos, sin], axis=1), jnp.concatenate([-sin, cos], axis=1)], axis=0
        )
        end = jnp.concatenate(
            [
                first[half * EDGE : (half + 1) * EDGE, part * EDGE : (part + 1) * EDGE].T
                for half in range(2)
            ],
            axis=1,
        )
        scale = jnp.bfloat16(1.0 / EDGE)
        for place in ((0, 1), (2,))[part]:
            rows = slice(2 * place * EDGE, 2 * (place + 1) * EDGE)
            second[rows, :] = ahead
            third[rows, :] = back * scale
            last[:, rows] = end * scale


def thirds(array, axis):
    high = array.astype(jnp.bfloat16)
    low = (array - high.astype(jnp.float32)).astype(jnp.bfloat16)
    return jnp.concatenate([high, low, high], axis=axis)


def dot(a, b):
    return jnp.dot(a, b, preferred_element_type=jnp.float32)


def pack_kernel(value_hbm, gate_hbm, filt_hbm, out_ref, held, arrived):
    slabs, _, chans, _ = out_ref.shape[1:]
    arrays = (value_hbm, gate_hbm, filt_hbm)

    def fetch(which, slab):
        rows = pl.ds(slab * EDGE, EDGE)
        return pltpu.make_async_copy(
            arrays[which].at[rows, :], held.at[which, rows, :], arrived.at[which, slab]
        )

    for slab in range(slabs):
        for which in range(3):
            fetch(which, slab).start()
    peers = EDGE // chans
    for slab in range(slabs):
        rows = slice(slab * EDGE, (slab + 1) * EDGE)
        for which in range(3):
            fetch(which, slab).wait()
        gated = held[0, rows].astype(jnp.float32) * held[1, rows].astype(jnp.float32)
        gated = gated.astype(jnp.bfloat16)
        for which, array in enumerate((gated, held[2, rows])):
            for part in range(array.shape[1] // EDGE):
                turned = array[:, part * EDGE : (part + 1) * EDGE].T
                out_ref[part * peers : (part + 1) * peers, slab, which] = turned.reshape(
                    peers, chans, EDGE
                )


def copy_all(copies):
    for copy in copies:
        copy.start()
    for copy in copies:
        copy.wait()


def deal_kernel(place, w_hbm, *rest):
    pieces, done = rest[:-1], rest[-1]
    copies = []
    for i, piece in enumerate(pieces):
        _, height, width = piece.shape
        target = lax.rem(place[0] + i + 1, ALONG_X)
        for side in range(2):
            col = (lax.rem(place[1] + side, 2) * ALONG_X + target) * width
            block = w_hbm.at[:, pl.ds(pl.multiple_of(col, width), width)]
            copies.append(pltpu.make_async_copy(block, piece.at[side], done.at[i, side]))
    for copy in copies:
        copy.start()
    for copy in copies:
        copy.wait()


def conv_kernel(
    chans, in_ref, first_table, base, turns, out_ref, wide, back, second, third, last
):
    build_tables(first_table, base, second, third, last)
    wide[...] = in_ref[...].astype(jnp.float32)
    cos, sin = turns[0], turns[1]

    @pl.loop(0, chans // BATCH, unroll=True)
    def _(step):
        first = step * BATCH
        signals = [
            wide[pl.ds(which * chans + first + k, EDGE, stride=2 * chans), :].astype(jnp.bfloat16)
            for k in range(BATCH)
            for which in range(2)
        ]
        both = jnp.concatenate(signals, axis=1)
        slow = dot(first_table[...], jnp.concatenate([both, both], axis=0))
        rows = []
        for k in range(2 * BATCH):
            cols = slice(k * EDGE, (k + 1) * EDGE)
            real, imag = slow[:EDGE, cols], slow[EDGE:, cols]
            rows.append(
                jnp.concatenate([real * cos + imag * sin, imag * cos - real * sin], axis=1)
            )
        spectra = dot(thirds(jnp.concatenate(rows, axis=0), 1), second[...])
        rows = []
        for k in range(BATCH):
            ours = spectra[2 * k * EDGE : (2 * k + 1) * EDGE]
            taps = spectra[(2 * k + 1) * EDGE : (2 * k + 2) * EDGE]
            ar, ai, br, bi = ours[:, :EDGE], ours[:, EDGE:], taps[:, :EDGE], taps[:, EDGE:]
            rows.append(jnp.concatenate([ar * br - ai * bi, ar * bi + ai * br], axis=1))
        wound = dot(thirds(jnp.concatenate(rows, axis=0), 1), third[...])
        cols = []
        for k in range(BATCH):
            real = wound[k * EDGE : (k + 1) * EDGE, :EDGE]
            imag = wound[k * EDGE : (k + 1) * EDGE, EDGE:]
            cols.append(
                jnp.concatenate([real * cos - imag * sin, imag * cos + real * sin], axis=0)
            )
        conv = dot(last[...], thirds(jnp.concatenate(cols, axis=1), 0))
        for k in range(BATCH):
            back[pl.ds(first + k, EDGE, stride=chans), :] = conv[:, k * EDGE : (k + 1) * EDGE]

    out_ref[...] = back[...].astype(jnp.bfloat16)


def mix_kernel(conv_ref, value_ref, gate_ref, gate_out_ref, skip_ref, *outs):
    slabs, chans = conv_ref.shape[1:3]
    width = value_ref.shape[1]
    peers = EDGE // chans
    for slab in range(slabs):
        rows = slice(slab * EDGE, (slab + 1) * EDGE)
        run, first = [(run, k) for run, count in enumerate(RUNS) for k in range(count)][slab]
        out_rows = slice(first * EDGE, (first + 1) * EDGE)
        for part in range(width // EDGE):
            cols = slice(part * EDGE, (part + 1) * EDGE)
            conv = conv_ref[part * peers : (part + 1) * peers, slab].reshape(EDGE, EDGE).T
            gated = gate_ref[rows, cols].astype(jnp.float32) * value_ref[rows, cols].astype(
                jnp.float32
            )
            gated = gated.astype(jnp.bfloat16).astype(jnp.float32)
            inner = conv.astype(jnp.float32) + skip_ref[:, cols] * gated
            mixed = gate_out_ref[rows, cols].astype(jnp.float32) * inner
            outs[run][out_rows, cols] = mixed.astype(jnp.bfloat16)


def project_kernel(*refs):
    *parts, weights, out_ref = refs

    def product(part, shift):
        return dot(part[...], weights[shift])

    total = product(parts[0], 0) + product(parts[1], ALONG_X - 1) + product(parts[-1], 1)
    across = jnp.concatenate([product(part, 2) for part in parts[-2:1:-1]], axis=0)
    out_ref[...] = (total + across).astype(out_ref.dtype)


def pack(value, gate_in, filt, groups):
    rows, width = value.shape
    slabs, chans = rows // EDGE, width // groups
    return pl.pallas_call(
        pack_kernel,
        in_specs=[pl.BlockSpec(memory_space=pl.ANY)] * 3,
        out_specs=pl.BlockSpec(memory_space=pltpu.VMEM),
        out_shape=jax.ShapeDtypeStruct((groups, slabs, 2, chans, EDGE), jnp.bfloat16),
        scratch_shapes=[
            pltpu.VMEM((3, rows, width), jnp.bfloat16),
            pltpu.SemaphoreType.DMA((3, slabs)),
        ],
        name="pack",
    )(value, gate_in, filt)


def deal(w_out, place, width):
    shape = jax.ShapeDtypeStruct((2, w_out.shape[0], width), jnp.bfloat16)
    return pl.pallas_call(
        deal_kernel,
        in_specs=[pl.BlockSpec(memory_space=pltpu.SMEM), pl.BlockSpec(memory_space=pl.ANY)],
        out_specs=[pl.BlockSpec(memory_space=pltpu.VMEM)] * ALONG_X,
        out_shape=[shape] * ALONG_X,
        scratch_shapes=[pltpu.SemaphoreType.DMA((ALONG_X, 2))],
        compiler_params=pltpu.CompilerParams(vmem_limit_bytes=WIDE),
        name="deal",
    )(place, w_out)


def convolve(spread, tables):
    groups, slabs, _, chans, _ = spread.shape
    rows = groups * slabs * chans
    whole = pl.BlockSpec(memory_space=pltpu.VMEM)
    conv = pl.pallas_call(
        functools.partial(conv_kernel, chans),
        in_specs=[whole] * (1 + len(tables)),
        out_specs=whole,
        out_shape=jax.ShapeDtypeStruct((rows, EDGE), jnp.bfloat16),
        scratch_shapes=[
            pltpu.VMEM((2 * rows, EDGE), jnp.float32),
            pltpu.VMEM((rows, EDGE), jnp.float32),
            pltpu.VMEM((6 * EDGE, 2 * EDGE), jnp.bfloat16),
            pltpu.VMEM((6 * EDGE, 2 * EDGE), jnp.bfloat16),
            pltpu.VMEM((EDGE, 6 * EDGE), jnp.bfloat16),
        ],
        compiler_params=pltpu.CompilerParams(vmem_limit_bytes=MEDIUM),
        cost_estimate=pl.CostEstimate(
            flops=6 * 10**9, bytes_accessed=2 * 10**6, transcendentals=0
        ),
        name="convolve",
    )(spread.reshape(2 * rows, EDGE), *tables)
    return conv.reshape(groups, slabs, chans, EDGE)


def mix(conv, value, gate_in, gate_out, skip):
    width = value.shape[1]
    whole = pl.BlockSpec(memory_space=pltpu.VMEM)
    return pl.pallas_call(
        mix_kernel,
        in_specs=[whole] * 5,
        out_specs=[whole] * len(RUNS),
        out_shape=[jax.ShapeDtypeStruct((run * EDGE, width), jnp.bfloat16) for run in RUNS],
        compiler_params=pltpu.CompilerParams(vmem_limit_bytes=SMALL),
        name="mix",
    )(conv, value, gate_in, gate_out, skip)


def stage_kernel(side, *refs):
    weights, out_ref, done = refs[:-2], refs[-2], refs[-1]
    copies = [
        pltpu.make_async_copy(weight.at[side], out_ref.at[shift], done.at[shift])
        for shift, weight in enumerate(weights)
    ]
    for copy in copies:
        copy.start()
    for copy in copies:
        copy.wait()


def stage(weights, side):
    return pl.pallas_call(
        functools.partial(stage_kernel, side),
        in_specs=[pl.BlockSpec(memory_space=pl.ANY)] * len(weights),
        out_specs=pl.BlockSpec(memory_space=pltpu.VMEM),
        out_shape=jax.ShapeDtypeStruct((len(weights), *weights[0].shape[1:]), jnp.bfloat16),
        scratch_shapes=[pltpu.SemaphoreType.DMA((len(weights),))],
        compiler_params=pltpu.CompilerParams(vmem_limit_bytes=SMALL),
        cost_estimate=pl.CostEstimate(flops=0, bytes_accessed=8 * 10**6, transcendentals=0),
        name="stage",
    )(*weights)


def project_half(parts, weights, dtype):
    rows, width = parts[0].shape
    whole = pl.BlockSpec(memory_space=pltpu.VMEM)
    return pl.pallas_call(
        project_kernel,
        in_specs=[whole] * (len(parts) + 1),
        out_specs=whole,
        out_shape=jax.ShapeDtypeStruct((rows, width), dtype),
        compiler_params=pltpu.CompilerParams(vmem_limit_bytes=SMALL),
        cost_estimate=pl.CostEstimate(
            flops=2 * rows * ALONG_X * width * width, bytes_accessed=3 * 10**6, transcendentals=0
        ),
        name="project",
    )(*parts, weights)


def along_x(shift):
    return [
        (i, i // ALONG_X * ALONG_X + (i + shift) % ALONG_X) for i in range(2 * ALONG_X)
    ]


def across_y():
    return [(i, (i + ALONG_X) % (2 * ALONG_X)) for i in range(2 * ALONG_X)]


def gather_x(own):
    def send(rows, shift):
        return lax.ppermute(rows, "chan", along_x(shift))

    before, after = send(own, 1), send(own, ALONG_X - 1)
    half = own.shape[0] // 2
    return [own, after, send(after[half:], ALONG_X - 1), send(before[:half], 1), before]


def per_device(value, gate_in, gate_out, filt, skip, w_out):
    groups = lax.axis_size("ctx")
    place = lax.axis_index("chan")
    where = jnp.stack([lax.rem(place, ALONG_X), lax.div(place, ALONG_X)])
    packed = pack(value, gate_in, filt, groups)
    *pieces, own = deal(w_out, where, value.shape[1])
    pieces = [lax.ppermute(piece, "chan", along_x(i + 1)) for i, piece in enumerate(pieces)]
    spread = lax.all_to_all(packed, "ctx", split_axis=0, concat_axis=0, tiled=True)
    tables = [jnp.asarray(table) for table in transform_tables()]
    conv = convolve(spread, tables)
    returned = lax.all_to_all(conv, "ctx", split_axis=0, concat_axis=0, tiled=True)
    mixed = mix(returned, value, gate_in, gate_out, skip[None])
    mixed, pieces = lax.optimization_barrier((mixed, pieces))
    parts = [gather_x(rows) for rows in mixed]
    weights = [own, *pieces]
    outs = []
    staged = stage(weights, 1)
    shares = [project_half(part, staged, jnp.bfloat16) for part in parts]
    theirs = [lax.ppermute(share, "chan", across_y()) for share in shares]
    weights, _ = lax.optimization_barrier((weights, shares))
    staged = stage(weights, 0)
    for part, arrived in zip(parts, theirs):
        mine = project_half(part, staged, jnp.float32)
        outs.append((mine + arrived.astype(jnp.float32)).astype(jnp.bfloat16))
    return jnp.concatenate(outs, axis=0)


def solution(mesh):
    placed = (
        P("ctx", "chan"),
        P("ctx", "chan"),
        P("ctx", "chan"),
        P("ctx", "chan"),
        P("chan"),
        P("chan", None),
    )
    return jax.shard_map(
        per_device, mesh=mesh, in_specs=placed, out_specs=P("ctx", "chan"), check_vma=False
    )
```

```python
import functools

import jax
import jax.numpy as jnp
import numpy as np
from jax import lax
from jax.experimental import pallas as pl
from jax.experimental.pallas import tpu as pltpu
from jax.sharding import PartitionSpec as P

EDGE = 128
WIDE = 48 * 1024 * 1024
MEDIUM = 32 * 1024 * 1024
SMALL = 16 * 1024 * 1024
ALONG_X = 4
RUNS = (2, 2)
BATCH = 8


def split_table(table):
    high = table.astype(jnp.bfloat16)
    low = (table - high.astype(np.float64)).astype(jnp.bfloat16)
    return high, low


@functools.cache
def transform_tables():
    steps = np.arange(EDGE)
    slow = 2.0 * np.pi * np.outer(steps + 0.25, steps) / EDGE
    fast = 2.0 * np.pi * np.outer(steps, steps) / EDGE
    turn = 2.0 * np.pi * np.outer(steps + 0.25, steps) / (EDGE * EDGE)
    first = np.concatenate([np.cos(slow), -np.sin(slow)], 0)
    second = np.concatenate([np.cos(fast), np.sin(fast)], 1)
    return (
        np.concatenate(split_table(first), 1),
        np.concatenate(split_table(second), 1),
        np.stack([np.cos(turn), np.sin(turn)]).astype(np.float32),
    )


def build_tables(first, base, second, third, last):
    for part in range(2):
        cos = base[:, 2 * part * EDGE : (2 * part + 1) * EDGE]
        sin = base[:, (2 * part + 1) * EDGE : (2 * part + 2) * EDGE]
        ahead = jnp.concatenate(
            [jnp.concatenate([cos, -sin], axis=1), jnp.concatenate([sin, cos], axis=1)], axis=0
        )
        back = jnp.concatenate(
            [jnp.concatenate([cos, sin], axis=1), jnp.concatenate([-sin, cos], axis=1)], axis=0
        )
        end = jnp.concatenate(
            [
                first[half * EDGE : (half + 1) * EDGE, part * EDGE : (part + 1) * EDGE].T
                for half in range(2)
            ],
            axis=1,
        )
        scale = jnp.bfloat16(1.0 / EDGE)
        for place in ((0, 1), (2,))[part]:
            rows = slice(2 * place * EDGE, 2 * (place + 1) * EDGE)
            second[rows, :] = ahead
            third[rows, :] = back * scale
            last[:, rows] = end * scale


def thirds(array, axis):
    high = array.astype(jnp.bfloat16)
    low = (array - high.astype(jnp.float32)).astype(jnp.bfloat16)
    return jnp.concatenate([high, low, high], axis=axis)


def dot(a, b):
    return jnp.dot(a, b, preferred_element_type=jnp.float32)


def pack_kernel(value_hbm, gate_hbm, filt_hbm, out_ref, held, arrived):
    slabs, _, chans, _ = out_ref.shape[1:]
    arrays = (value_hbm, gate_hbm, filt_hbm)

    def fetch(which, slab):
        rows = pl.ds(slab * EDGE, EDGE)
        return pltpu.make_async_copy(
            arrays[which].at[rows, :], held.at[which, rows, :], arrived.at[which, slab]
        )

    for slab in range(slabs):
        for which in range(3):
            fetch(which, slab).start()
    peers = EDGE // chans
    for slab in range(slabs):
        rows = slice(slab * EDGE, (slab + 1) * EDGE)
        for which in range(3):
            fetch(which, slab).wait()
        gated = held[0, rows].astype(jnp.float32) * held[1, rows].astype(jnp.float32)
        gated = gated.astype(jnp.bfloat16)
        for which, array in enumerate((gated, held[2, rows])):
            for part in range(array.shape[1] // EDGE):
                turned = array[:, part * EDGE : (part + 1) * EDGE].T
                out_ref[part * peers : (part + 1) * peers, slab, which] = turned.reshape(
                    peers, chans, EDGE
                )


def copy_all(copies):
    for copy in copies:
        copy.start()
    for copy in copies:
        copy.wait()


def deal_kernel(place, w_hbm, *rest):
    pieces, done = rest[:-1], rest[-1]
    copies = []
    for i, piece in enumerate(pieces):
        _, height, width = piece.shape
        target = lax.rem(place[0] + i + 1, ALONG_X)
        for side in range(2):
            col = (lax.rem(place[1] + side, 2) * ALONG_X + target) * width
            block = w_hbm.at[:, pl.ds(pl.multiple_of(col, width), width)]
            copies.append(pltpu.make_async_copy(block, piece.at[side], done.at[i, side]))
    for copy in copies:
        copy.start()
    for copy in copies:
        copy.wait()


def conv_kernel(
    chans, in_ref, first_table, base, turns, out_ref, wide, back, second, third, last
):
    build_tables(first_table, base, second, third, last)
    wide[...] = in_ref[...].astype(jnp.float32)
    cos, sin = turns[0], turns[1]

    for first in range(0, chans, BATCH):
        signals = [
            wide[pl.ds(which * chans + first + k, EDGE, stride=2 * chans), :].astype(jnp.bfloat16)
            for k in range(BATCH)
            for which in range(2)
        ]
        both = jnp.concatenate(signals, axis=1)
        slow = dot(first_table[...], jnp.concatenate([both, both], axis=0))
        rows = []
        for k in range(2 * BATCH):
            cols = slice(k * EDGE, (k + 1) * EDGE)
            real, imag = slow[:EDGE, cols], slow[EDGE:, cols]
            rows.append(
                jnp.concatenate([real * cos + imag * sin, imag * cos - real * sin], axis=1)
            )
        spectra = dot(thirds(jnp.concatenate(rows, axis=0), 1), second[...])
        rows = []
        for k in range(BATCH):
            ours = spectra[2 * k * EDGE : (2 * k + 1) * EDGE]
            taps = spectra[(2 * k + 1) * EDGE : (2 * k + 2) * EDGE]
            ar, ai, br, bi = ours[:, :EDGE], ours[:, EDGE:], taps[:, :EDGE], taps[:, EDGE:]
            rows.append(jnp.concatenate([ar * br - ai * bi, ar * bi + ai * br], axis=1))
        wound = dot(thirds(jnp.concatenate(rows, axis=0), 1), third[...])
        cols = []
        for k in range(BATCH):
            real = wound[k * EDGE : (k + 1) * EDGE, :EDGE]
            imag = wound[k * EDGE : (k + 1) * EDGE, EDGE:]
            cols.append(
                jnp.concatenate([real * cos - imag * sin, imag * cos + real * sin], axis=0)
            )
        conv = dot(last[...], thirds(jnp.concatenate(cols, axis=1), 0))
        for k in range(BATCH):
            back[pl.ds(first + k, EDGE, stride=chans), :] = conv[:, k * EDGE : (k + 1) * EDGE]

    out_ref[...] = back[...].astype(jnp.bfloat16)


def mix_kernel(conv_ref, value_ref, gate_ref, gate_out_ref, skip_ref, *outs):
    slabs, chans = conv_ref.shape[1:3]
    width = value_ref.shape[1]
    peers = EDGE // chans
    for slab in range(slabs):
        rows = slice(slab * EDGE, (slab + 1) * EDGE)
        run, first = [(run, k) for run, count in enumerate(RUNS) for k in range(count)][slab]
        out_rows = slice(first * EDGE, (first + 1) * EDGE)
        for part in range(width // EDGE):
            cols = slice(part * EDGE, (part + 1) * EDGE)
            conv = conv_ref[part * peers : (part + 1) * peers, slab].reshape(EDGE, EDGE).T
            gated = gate_ref[rows, cols].astype(jnp.float32) * value_ref[rows, cols].astype(
                jnp.float32
            )
            gated = gated.astype(jnp.bfloat16).astype(jnp.float32)
            inner = conv.astype(jnp.float32) + skip_ref[:, cols] * gated
            mixed = gate_out_ref[rows, cols].astype(jnp.float32) * inner
            outs[run][out_rows, cols] = mixed.astype(jnp.bfloat16)


def project_kernel(*refs):
    *parts, weights, out_ref = refs

    def product(part, shift):
        return dot(part[...], weights[shift])

    total = product(parts[0], 0) + product(parts[1], ALONG_X - 1) + product(parts[-1], 1)
    across = jnp.concatenate([product(part, 2) for part in parts[-2:1:-1]], axis=0)
    out_ref[...] = (total + across).astype(out_ref.dtype)


def pack(value, gate_in, filt, groups):
    rows, width = value.shape
    slabs, chans = rows // EDGE, width // groups
    return pl.pallas_call(
        pack_kernel,
        in_specs=[pl.BlockSpec(memory_space=pl.ANY)] * 3,
        out_specs=pl.BlockSpec(memory_space=pltpu.VMEM),
        out_shape=jax.ShapeDtypeStruct((groups, slabs, 2, chans, EDGE), jnp.bfloat16),
        scratch_shapes=[
            pltpu.VMEM((3, rows, width), jnp.bfloat16),
            pltpu.SemaphoreType.DMA((3, slabs)),
        ],
        name="pack",
    )(value, gate_in, filt)


def deal(w_out, place, width):
    shape = jax.ShapeDtypeStruct((2, w_out.shape[0], width), jnp.bfloat16)
    return pl.pallas_call(
        deal_kernel,
        in_specs=[pl.BlockSpec(memory_space=pltpu.SMEM), pl.BlockSpec(memory_space=pl.ANY)],
        out_specs=[pl.BlockSpec(memory_space=pltpu.VMEM)] * ALONG_X,
        out_shape=[shape] * ALONG_X,
        scratch_shapes=[pltpu.SemaphoreType.DMA((ALONG_X, 2))],
        compiler_params=pltpu.CompilerParams(vmem_limit_bytes=WIDE),
        name="deal",
    )(place, w_out)


def convolve(spread, tables):
    groups, slabs, _, chans, _ = spread.shape
    rows = groups * slabs * chans
    whole = pl.BlockSpec(memory_space=pltpu.VMEM)
    conv = pl.pallas_call(
        functools.partial(conv_kernel, chans),
        in_specs=[whole] * (1 + len(tables)),
        out_specs=whole,
        out_shape=jax.ShapeDtypeStruct((rows, EDGE), jnp.bfloat16),
        scratch_shapes=[
            pltpu.VMEM((2 * rows, EDGE), jnp.float32),
            pltpu.VMEM((rows, EDGE), jnp.float32),
            pltpu.VMEM((6 * EDGE, 2 * EDGE), jnp.bfloat16),
            pltpu.VMEM((6 * EDGE, 2 * EDGE), jnp.bfloat16),
            pltpu.VMEM((EDGE, 6 * EDGE), jnp.bfloat16),
        ],
        compiler_params=pltpu.CompilerParams(vmem_limit_bytes=MEDIUM),
        cost_estimate=pl.CostEstimate(
            flops=6 * 10**9, bytes_accessed=2 * 10**6, transcendentals=0
        ),
        name="convolve",
    )(spread.reshape(2 * rows, EDGE), *tables)
    return conv.reshape(groups, slabs, chans, EDGE)


def mix(conv, value, gate_in, gate_out, skip):
    width = value.shape[1]
    whole = pl.BlockSpec(memory_space=pltpu.VMEM)
    return pl.pallas_call(
        mix_kernel,
        in_specs=[whole] * 5,
        out_specs=[whole] * len(RUNS),
        out_shape=[jax.ShapeDtypeStruct((run * EDGE, width), jnp.bfloat16) for run in RUNS],
        compiler_params=pltpu.CompilerParams(vmem_limit_bytes=SMALL),
        name="mix",
    )(conv, value, gate_in, gate_out, skip)


def stage_kernel(side, *refs):
    weights, out_ref, done = refs[:-2], refs[-2], refs[-1]
    copies = [
        pltpu.make_async_copy(weight.at[side], out_ref.at[shift], done.at[shift])
        for shift, weight in enumerate(weights)
    ]
    for copy in copies:
        copy.start()
    for copy in copies:
        copy.wait()


def stage(weights, side):
    return pl.pallas_call(
        functools.partial(stage_kernel, side),
        in_specs=[pl.BlockSpec(memory_space=pl.ANY)] * len(weights),
        out_specs=pl.BlockSpec(memory_space=pltpu.VMEM),
        out_shape=jax.ShapeDtypeStruct((len(weights), *weights[0].shape[1:]), jnp.bfloat16),
        scratch_shapes=[pltpu.SemaphoreType.DMA((len(weights),))],
        compiler_params=pltpu.CompilerParams(vmem_limit_bytes=SMALL),
        cost_estimate=pl.CostEstimate(flops=0, bytes_accessed=8 * 10**6, transcendentals=0),
        name="stage",
    )(*weights)


def project_half(parts, weights, dtype):
    rows, width = parts[0].shape
    whole = pl.BlockSpec(memory_space=pltpu.VMEM)
    return pl.pallas_call(
        project_kernel,
        in_specs=[whole] * (len(parts) + 1),
        out_specs=whole,
        out_shape=jax.ShapeDtypeStruct((rows, width), dtype),
        compiler_params=pltpu.CompilerParams(vmem_limit_bytes=SMALL),
        cost_estimate=pl.CostEstimate(
            flops=2 * rows * ALONG_X * width * width, bytes_accessed=3 * 10**6, transcendentals=0
        ),
        name="project",
    )(*parts, weights)


def along_x(shift):
    return [
        (i, i // ALONG_X * ALONG_X + (i + shift) % ALONG_X) for i in range(2 * ALONG_X)
    ]


def across_y():
    return [(i, (i + ALONG_X) % (2 * ALONG_X)) for i in range(2 * ALONG_X)]


def gather_x(own):
    def send(rows, shift):
        return lax.ppermute(rows, "chan", along_x(shift))

    before, after = send(own, 1), send(own, ALONG_X - 1)
    half = own.shape[0] // 2
    return [own, after, send(after[half:], ALONG_X - 1), send(before[:half], 1), before]


def per_device(value, gate_in, gate_out, filt, skip, w_out):
    groups = lax.axis_size("ctx")
    place = lax.axis_index("chan")
    where = jnp.stack([lax.rem(place, ALONG_X), lax.div(place, ALONG_X)])
    packed = pack(value, gate_in, filt, groups)
    *pieces, own = deal(w_out, where, value.shape[1])
    pieces = [lax.ppermute(piece, "chan", along_x(i + 1)) for i, piece in enumerate(pieces)]
    spread = lax.all_to_all(packed, "ctx", split_axis=0, concat_axis=0, tiled=True)
    tables = [jnp.asarray(table) for table in transform_tables()]
    conv = convolve(spread, tables)
    returned = lax.all_to_all(conv, "ctx", split_axis=0, concat_axis=0, tiled=True)
    mixed = mix(returned, value, gate_in, gate_out, skip[None])
    mixed, pieces = lax.optimization_barrier((mixed, pieces))
    parts = [gather_x(rows) for rows in mixed]
    weights = [own, *pieces]
    outs = []
    staged = stage(weights, 1)
    shares = [project_half(part, staged, jnp.bfloat16) for part in parts]
    theirs = [lax.ppermute(share, "chan", across_y()) for share in shares]
    weights, _ = lax.optimization_barrier((weights, shares))
    staged = stage(weights, 0)
    for part, arrived in zip(parts, theirs):
        mine = project_half(part, staged, jnp.float32)
        outs.append((mine + arrived.astype(jnp.float32)).astype(jnp.bfloat16))
    return jnp.concatenate(outs, axis=0)


def solution(mesh):
    placed = (
        P("ctx", "chan"),
        P("ctx", "chan"),
        P("ctx", "chan"),
        P("ctx", "chan"),
        P("chan"),
        P("chan", None),
    )
    return jax.shard_map(
        per_device, mesh=mesh, in_specs=placed, out_specs=P("ctx", "chan"), check_vma=False
    )
```

```python
import functools

import jax
import jax.numpy as jnp
import numpy as np
from jax import lax
from jax.experimental import pallas as pl
from jax.experimental.pallas import tpu as pltpu
from jax.sharding import PartitionSpec as P

EDGE = 128
WIDE = 48 * 1024 * 1024
MEDIUM = 32 * 1024 * 1024
SMALL = 16 * 1024 * 1024
ALONG_X = 4
RUNS = (2, 2)
BATCH = 8


def split_table(table):
    high = table.astype(jnp.bfloat16)
    low = (table - high.astype(np.float64)).astype(jnp.bfloat16)
    return high, low


@functools.cache
def transform_tables():
    steps = np.arange(EDGE)
    slow = 2.0 * np.pi * np.outer(steps + 0.25, steps) / EDGE
    fast = 2.0 * np.pi * np.outer(steps, steps) / EDGE
    turn = 2.0 * np.pi * np.outer(steps + 0.25, steps) / (EDGE * EDGE)
    first = np.concatenate([np.cos(slow), -np.sin(slow)], 0)
    second = np.concatenate([np.cos(fast), np.sin(fast)], 1)
    return (
        np.concatenate(split_table(first), 1),
        np.concatenate(split_table(second), 1),
        np.stack([np.cos(turn), np.sin(turn)]).astype(np.float32),
    )


def build_tables(first, base, second, third, last):
    for part in range(2):
        cos = base[:, 2 * part * EDGE : (2 * part + 1) * EDGE]
        sin = base[:, (2 * part + 1) * EDGE : (2 * part + 2) * EDGE]
        ahead = jnp.concatenate(
            [jnp.concatenate([cos, -sin], axis=1), jnp.concatenate([sin, cos], axis=1)], axis=0
        )
        back = jnp.concatenate(
            [jnp.concatenate([cos, sin], axis=1), jnp.concatenate([-sin, cos], axis=1)], axis=0
        )
        end = jnp.concatenate(
            [
                first[half * EDGE : (half + 1) * EDGE, part * EDGE : (part + 1) * EDGE].T
                for half in range(2)
            ],
            axis=1,
        )
        scale = jnp.bfloat16(1.0 / EDGE)
        last[part * EDGE : (part + 1) * EDGE, :] = end * scale
        for place in ((0, 1), (2,))[part]:
            rows = slice(2 * place * EDGE, 2 * (place + 1) * EDGE)
            second[rows, :] = ahead
            third[rows, :] = back * scale


def halves(array):
    high = array.astype(jnp.bfloat16)
    return high, (array - high.astype(jnp.float32)).astype(jnp.bfloat16)


def thirds(array, axis):
    high, low = halves(array)
    return jnp.concatenate([high, low, high], axis=axis)


def dot(a, b):
    return jnp.dot(a, b, preferred_element_type=jnp.float32)


def pack_kernel(value_hbm, gate_hbm, filt_hbm, out_ref, held, arrived):
    slabs, _, chans, _ = out_ref.shape[1:]
    arrays = (value_hbm, gate_hbm, filt_hbm)

    def fetch(which, slab):
        rows = pl.ds(slab * EDGE, EDGE)
        return pltpu.make_async_copy(
            arrays[which].at[rows, :], held.at[which, rows, :], arrived.at[which, slab]
        )

    for slab in range(slabs):
        for which in range(3):
            fetch(which, slab).start()
    peers = EDGE // chans
    for slab in range(slabs):
        rows = slice(slab * EDGE, (slab + 1) * EDGE)
        for which in range(3):
            fetch(which, slab).wait()
        gated = held[0, rows].astype(jnp.float32) * held[1, rows].astype(jnp.float32)
        gated = gated.astype(jnp.bfloat16)
        for which, array in enumerate((gated, held[2, rows])):
            for part in range(array.shape[1] // EDGE):
                turned = array[:, part * EDGE : (part + 1) * EDGE].T
                out_ref[part * peers : (part + 1) * peers, slab, which] = turned.reshape(
                    peers, chans, EDGE
                )


def copy_all(copies):
    for copy in copies:
        copy.start()
    for copy in copies:
        copy.wait()


def deal_kernel(place, w_hbm, *rest):
    pieces, done = rest[:-1], rest[-1]
    copies = []
    for i, piece in enumerate(pieces):
        _, height, width = piece.shape
        target = lax.rem(place[0] + i + 1, ALONG_X)
        for side in range(2):
            col = (lax.rem(place[1] + side, 2) * ALONG_X + target) * width
            block = w_hbm.at[:, pl.ds(pl.multiple_of(col, width), width)]
            copies.append(pltpu.make_async_copy(block, piece.at[side], done.at[i, side]))
    for copy in copies:
        copy.start()
    for copy in copies:
        copy.wait()


def conv_kernel(
    chans, in_ref, first_table, base, turns, out_ref, wide, back, second, third, last
):
    build_tables(first_table, base, second, third, last)
    wide[...] = in_ref[...].astype(jnp.float32)
    cos, sin = turns[0], turns[1]

    for first in range(0, chans, BATCH):
        signals = [
            wide[pl.ds(which * chans + first + k, EDGE, stride=2 * chans), :].astype(jnp.bfloat16)
            for k in range(BATCH)
            for which in range(2)
        ]
        both = jnp.concatenate(signals, axis=1)
        slow = dot(first_table[...], jnp.concatenate([both, both], axis=0))
        rows = []
        for k in range(2 * BATCH):
            cols = slice(k * EDGE, (k + 1) * EDGE)
            real, imag = slow[:EDGE, cols], slow[EDGE:, cols]
            rows.append(
                jnp.concatenate([real * cos + imag * sin, imag * cos - real * sin], axis=1)
            )
        spectra = dot(thirds(jnp.concatenate(rows, axis=0), 1), second[...])
        rows = []
        for k in range(BATCH):
            ours = spectra[2 * k * EDGE : (2 * k + 1) * EDGE]
            taps = spectra[(2 * k + 1) * EDGE : (2 * k + 2) * EDGE]
            ar, ai, br, bi = ours[:, :EDGE], ours[:, EDGE:], taps[:, :EDGE], taps[:, EDGE:]
            rows.append(jnp.concatenate([ar * br - ai * bi, ar * bi + ai * br], axis=1))
        wound = dot(thirds(jnp.concatenate(rows, axis=0), 1), third[...])
        cols = []
        for k in range(BATCH):
            real = wound[k * EDGE : (k + 1) * EDGE, :EDGE]
            imag = wound[k * EDGE : (k + 1) * EDGE, EDGE:]
            cols.append(
                jnp.concatenate([real * cos - imag * sin, imag * cos + real * sin], axis=0)
            )
        high, low = halves(jnp.concatenate(cols, axis=1))
        both = dot(last[...], high)
        conv = both[:EDGE] + both[EDGE:] + dot(last[:EDGE, :], low)
        for k in range(BATCH):
            back[pl.ds(first + k, EDGE, stride=chans), :] = conv[:, k * EDGE : (k + 1) * EDGE]

    out_ref[...] = back[...].astype(jnp.bfloat16)


def mix_kernel(conv_ref, value_ref, gate_ref, gate_out_ref, skip_ref, *outs):
    slabs, chans = conv_ref.shape[1:3]
    width = value_ref.shape[1]
    peers = EDGE // chans
    for slab in range(slabs):
        rows = slice(slab * EDGE, (slab + 1) * EDGE)
        run, first = [(run, k) for run, count in enumerate(RUNS) for k in range(count)][slab]
        out_rows = slice(first * EDGE, (first + 1) * EDGE)
        for part in range(width // EDGE):
            cols = slice(part * EDGE, (part + 1) * EDGE)
            conv = conv_ref[part * peers : (part + 1) * peers, slab].reshape(EDGE, EDGE).T
            gated = gate_ref[rows, cols].astype(jnp.float32) * value_ref[rows, cols].astype(
                jnp.float32
            )
            gated = gated.astype(jnp.bfloat16).astype(jnp.float32)
            inner = conv.astype(jnp.float32) + skip_ref[:, cols] * gated
            mixed = gate_out_ref[rows, cols].astype(jnp.float32) * inner
            outs[run][out_rows, cols] = mixed.astype(jnp.bfloat16)


def project_kernel(*refs):
    *parts, weights, out_ref = refs

    def product(part, shift):
        return dot(part[...], weights[shift])

    total = product(parts[0], 0) + product(parts[1], ALONG_X - 1) + product(parts[-1], 1)
    across = jnp.concatenate([product(part, 2) for part in parts[-2:1:-1]], axis=0)
    out_ref[...] = (total + across).astype(out_ref.dtype)


def pack(value, gate_in, filt, groups):
    rows, width = value.shape
    slabs, chans = rows // EDGE, width // groups
    return pl.pallas_call(
        pack_kernel,
        in_specs=[pl.BlockSpec(memory_space=pl.ANY)] * 3,
        out_specs=pl.BlockSpec(memory_space=pltpu.VMEM),
        out_shape=jax.ShapeDtypeStruct((groups, slabs, 2, chans, EDGE), jnp.bfloat16),
        scratch_shapes=[
            pltpu.VMEM((3, rows, width), jnp.bfloat16),
            pltpu.SemaphoreType.DMA((3, slabs)),
        ],
        name="pack",
    )(value, gate_in, filt)


def deal(w_out, place, width):
    shape = jax.ShapeDtypeStruct((2, w_out.shape[0], width), jnp.bfloat16)
    return pl.pallas_call(
        deal_kernel,
        in_specs=[pl.BlockSpec(memory_space=pltpu.SMEM), pl.BlockSpec(memory_space=pl.ANY)],
        out_specs=[pl.BlockSpec(memory_space=pltpu.VMEM)] * ALONG_X,
        out_shape=[shape] * ALONG_X,
        scratch_shapes=[pltpu.SemaphoreType.DMA((ALONG_X, 2))],
        compiler_params=pltpu.CompilerParams(vmem_limit_bytes=WIDE),
        name="deal",
    )(place, w_out)


def convolve(spread, tables):
    groups, slabs, _, chans, _ = spread.shape
    rows = groups * slabs * chans
    whole = pl.BlockSpec(memory_space=pltpu.VMEM)
    conv = pl.pallas_call(
        functools.partial(conv_kernel, chans),
        in_specs=[whole] * (1 + len(tables)),
        out_specs=whole,
        out_shape=jax.ShapeDtypeStruct((rows, EDGE), jnp.bfloat16),
        scratch_shapes=[
            pltpu.VMEM((2 * rows, EDGE), jnp.float32),
            pltpu.VMEM((rows, EDGE), jnp.float32),
            pltpu.VMEM((6 * EDGE, 2 * EDGE), jnp.bfloat16),
            pltpu.VMEM((6 * EDGE, 2 * EDGE), jnp.bfloat16),
            pltpu.VMEM((2 * EDGE, 2 * EDGE), jnp.bfloat16),
        ],
        compiler_params=pltpu.CompilerParams(vmem_limit_bytes=MEDIUM),
        cost_estimate=pl.CostEstimate(
            flops=6 * 10**9, bytes_accessed=2 * 10**6, transcendentals=0
        ),
        name="convolve",
    )(spread.reshape(2 * rows, EDGE), *tables)
    return conv.reshape(groups, slabs, chans, EDGE)


def mix(conv, value, gate_in, gate_out, skip):
    width = value.shape[1]
    whole = pl.BlockSpec(memory_space=pltpu.VMEM)
    return pl.pallas_call(
        mix_kernel,
        in_specs=[whole] * 5,
        out_specs=[whole] * len(RUNS),
        out_shape=[jax.ShapeDtypeStruct((run * EDGE, width), jnp.bfloat16) for run in RUNS],
        compiler_params=pltpu.CompilerParams(vmem_limit_bytes=SMALL),
        name="mix",
    )(conv, value, gate_in, gate_out, skip)


def stage_kernel(side, *refs):
    weights, out_ref, done = refs[:-2], refs[-2], refs[-1]
    copies = [
        pltpu.make_async_copy(weight.at[side], out_ref.at[shift], done.at[shift])
        for shift, weight in enumerate(weights)
    ]
    for copy in copies:
        copy.start()
    for copy in copies:
        copy.wait()


def stage(weights, side):
    return pl.pallas_call(
        functools.partial(stage_kernel, side),
        in_specs=[pl.BlockSpec(memory_space=pl.ANY)] * len(weights),
        out_specs=pl.BlockSpec(memory_space=pltpu.VMEM),
        out_shape=jax.ShapeDtypeStruct((len(weights), *weights[0].shape[1:]), jnp.bfloat16),
        scratch_shapes=[pltpu.SemaphoreType.DMA((len(weights),))],
        compiler_params=pltpu.CompilerParams(vmem_limit_bytes=SMALL),
        cost_estimate=pl.CostEstimate(flops=0, bytes_accessed=8 * 10**6, transcendentals=0),
        name="stage",
    )(*weights)


def project_half(parts, weights, dtype):
    rows, width = parts[0].shape
    whole = pl.BlockSpec(memory_space=pltpu.VMEM)
    return pl.pallas_call(
        project_kernel,
        in_specs=[whole] * (len(parts) + 1),
        out_specs=whole,
        out_shape=jax.ShapeDtypeStruct((rows, width), dtype),
        compiler_params=pltpu.CompilerParams(vmem_limit_bytes=SMALL),
        cost_estimate=pl.CostEstimate(
            flops=2 * rows * ALONG_X * width * width, bytes_accessed=3 * 10**6, transcendentals=0
        ),
        name="project",
    )(*parts, weights)


def along_x(shift):
    return [
        (i, i // ALONG_X * ALONG_X + (i + shift) % ALONG_X) for i in range(2 * ALONG_X)
    ]


def across_y():
    return [(i, (i + ALONG_X) % (2 * ALONG_X)) for i in range(2 * ALONG_X)]


def gather_x(own):
    def send(rows, shift):
        return lax.ppermute(rows, "chan", along_x(shift))

    before, after = send(own, 1), send(own, ALONG_X - 1)
    half = own.shape[0] // 2
    return [own, after, send(after[half:], ALONG_X - 1), send(before[:half], 1), before]


def per_device(value, gate_in, gate_out, filt, skip, w_out):
    groups = lax.axis_size("ctx")
    place = lax.axis_index("chan")
    where = jnp.stack([lax.rem(place, ALONG_X), lax.div(place, ALONG_X)])
    packed = pack(value, gate_in, filt, groups)
    *pieces, own = deal(w_out, where, value.shape[1])
    pieces = [lax.ppermute(piece, "chan", along_x(i + 1)) for i, piece in enumerate(pieces)]
    spread = lax.all_to_all(packed, "ctx", split_axis=0, concat_axis=0, tiled=True)
    tables = [jnp.asarray(table) for table in transform_tables()]
    conv = convolve(spread, tables)
    returned = lax.all_to_all(conv, "ctx", split_axis=0, concat_axis=0, tiled=True)
    mixed = mix(returned, value, gate_in, gate_out, skip[None])
    mixed, pieces = lax.optimization_barrier((mixed, pieces))
    parts = [gather_x(rows) for rows in mixed]
    weights = [own, *pieces]
    outs = []
    staged = stage(weights, 1)
    shares = [project_half(part, staged, jnp.bfloat16) for part in parts]
    theirs = [lax.ppermute(share, "chan", across_y()) for share in shares]
    weights, _ = lax.optimization_barrier((weights, shares))
    staged = stage(weights, 0)
    for part, arrived in zip(parts, theirs):
        mine = project_half(part, staged, jnp.float32)
        outs.append((mine + arrived.astype(jnp.float32)).astype(jnp.bfloat16))
    return jnp.concatenate(outs, axis=0)


def solution(mesh):
    placed = (
        P("ctx", "chan"),
        P("ctx", "chan"),
        P("ctx", "chan"),
        P("ctx", "chan"),
        P("chan"),
        P("chan", None),
    )
    return jax.shard_map(
        per_device, mesh=mesh, in_specs=placed, out_specs=P("ctx", "chan"), check_vma=False
    )
```
